128 devices in a mesh: dp: 16 (over z, y_hi, core), ctx: 8 (over y_lo, x).
Axes of the slice: x: 4, y: 4 (y_hi: 2, y_lo: 2; y = y_hi * 2 + y_lo), z: 4, core: 2. Of those that a mesh axis runs over, the one named last changes fastest.
Arguments:
- tokens: float32 [16, 2048, 1408], P('dp', 'ctx'), may hold values from -6 to 6
- counts: int32 [16, 8], P('dp', 'ctx'), may hold values from 64 to 256, as said below
- w_qkv: float32 [1408, 2112], replicated
- w_out: float32 [704, 1408], replicated, may hold values from -0.21875 to 0.21875
- cotangent: float32 [16, 2048, 1408], P('dp', 'ctx'), may hold values from -6 to 6
Outputs:
- mixed: float32 [16, 2048, 1408], P('dp', 'ctx')
- grad_tokens: float32 [16, 2048, 1408], P('dp', 'ctx')
- grad_qkv: float32 [1408, 2112], P(('dp', 'ctx'))
- grad_out: float32 [704, 1408], P(None, ('dp', 'ctx'))
The draws below stay inside these ranges and needn't reach their ends.
Inputs may be any that keep to these rules, and one draw needn't show every extreme that they name: `counts`: in every clip one device holds exactly 256 visible rows.
All inputs are finite; a program needn't handle non-finite values.
Results may differ from the reference program's by a relative error of at most 0.0003.
Values sent between devices are 32-bit elements; how exact they have to be, the bound alone decides.
No kernel may reach another device: no remote copies, remote signals or barrier semaphores. Data moves between devices by JAX's collectives and lax.ppermute only.
A program may use at most 192 MiB of HBM per device.

```python
import jax
import jax.numpy as jnp
from jax import lax

D = 1408
HEADS = 8
HEAD_DIM = 88
CAP = 256
HD = 704
CLIPS = 16
CTXS = 8
ROWS = 2048


def draw_counts(key, part):
    key = jax.random.fold_in(key, 5)
    first = jax.random.fold_in(key, 1)
    second = jax.random.fold_in(key, 2)
    drawn = jax.random.randint(first, (CLIPS, CTXS), CAP // 4, CAP + 1)
    fullest = jax.random.randint(second, (CLIPS,), 0, CTXS)
    chosen = jnp.arange(CTXS)[None, :] == fullest[:, None]
    return jnp.where(chosen, CAP, drawn).astype(jnp.int32)


def draw_w_qkv(key, part):
    key = jax.random.fold_in(key, 11)
    width = HEADS * HEAD_DIM
    base = jnp.clip(jax.random.normal(key, (D, 3 * width), jnp.float32), -4.0, 4.0) * D ** (-0.5)
    return base


def block_scale(own_key, dims, cuts, smallest, top_value):
    def one(dim, shards_of):
        heights = jax.random.uniform(jax.random.fold_in(jax.random.fold_in(own_key, 6), dim), (shards_of,), jnp.float32, smallest / len(cuts), top_value / len(cuts))
        return jnp.repeat(jnp.exp(heights), dims[dim] // shards_of).reshape((-1,) + (1,) * (len(dims) - dim - 1))

    factor_of = one(*cuts[0])
    for cut in cuts[1:]:
        factor_of = factor_of * one(*cut)
    return factor_of


def gaussian(key, shape, scale, most, cuts=(), held_as=jnp.bfloat16):
    factor_of = block_scale(key, shape, cuts, -0.22, 0.18) if cuts else 1.0
    result = jax.random.normal(key, shape, jnp.float32) * scale * factor_of
    return jnp.minimum(jnp.maximum(result, -most), most).astype(held_as)


def setup_inputs(seed: int = 0) -> dict:
    splits = jax.random.split(jax.random.key(seed), 6)
    tokens = gaussian(splits[0], (CLIPS, ROWS, D), 1.0, 6.0, ((0, 16), (1, 8)), jnp.float32)
    counts = draw_counts(jax.random.fold_in(splits[5], 71), 0)
    w_qkv = draw_w_qkv(jax.random.fold_in(splits[5], 71), 0)
    w_out = gaussian(splits[3], (HD, D), HD ** -0.5, 0.21875, (), jnp.float32)
    cotangent = gaussian(splits[4], (CLIPS, ROWS, D), 1.0, 6.0, ((0, 16), (1, 8)), jnp.float32)
    return dict(tokens=tokens, counts=counts, w_qkv=w_qkv, w_out=w_out, cotangent=cotangent)


HIGH = lax.Precision.HIGHEST

def clip_layer(x, count, w_qkv, w_out):
    rows = jnp.arange(ROWS)
    owner = rows // CAP
    slot = rows % CAP
    limit = lax.optimization_barrier(jnp.sum(jnp.where(owner[:, None] == jnp.arange(CTXS)[None, :], count[None, :], 0), axis=1))
    valid = (slot < limit).astype(jnp.float32)
    mean = lax.optimization_barrier(jnp.mean(x, axis=-1, keepdims=True))
    centred = x - mean
    var = lax.optimization_barrier(jnp.mean(centred * centred, axis=-1, keepdims=True))
    normed = centred * lax.rsqrt(var + 1e-06)
    qkv = jnp.dot(normed, w_qkv, precision=HIGH)
    width = HEADS * HEAD_DIM
    query = qkv[:, :width].reshape(ROWS, HEADS, HEAD_DIM)
    keys = qkv[:, width:2 * width].reshape(ROWS, HEADS, HEAD_DIM)
    values = qkv[:, 2 * width:].reshape(ROWS, HEADS, HEAD_DIM)
    scores = jnp.einsum('qhd,khd->hqk', query, keys, precision=HIGH) / jnp.sqrt(jnp.float32(HEAD_DIM))
    live = valid[None, None, :] > 0
    top = lax.stop_gradient(lax.optimization_barrier(jnp.max(jnp.where(live, scores, -jnp.inf), axis=-1, keepdims=True)))
    expo = jnp.exp(jnp.where(live, scores - top, 0.0)) * valid[None, None, :]
    probs = expo / lax.optimization_barrier(jnp.sum(expo, axis=-1, keepdims=True))
    attended = jnp.einsum('hqk,khd->qhd', probs, values, precision=HIGH).reshape(ROWS, width)
    proj = jnp.dot(attended, w_out, precision=HIGH)
    return valid[:, None] * (x + proj)

def reference(tokens, counts, w_qkv, w_out, cotangent):

    def step(carry, item):
        x, count, grad = item
        mixed, pull = jax.vjp(lambda a, b, c: clip_layer(a, count, b, c), x, w_qkv, w_out)
        gx, gq, go = pull(grad)
        return ((carry[0] + gq, carry[1] + go), (mixed, gx))
    start = (jnp.zeros(w_qkv.shape, jnp.float32), jnp.zeros(w_out.shape, jnp.float32))
    totals, outs = lax.scan(step, start, (tokens, counts, cotangent))
    return (outs[0], outs[1], totals[0], totals[1])
```

```python
import functools

import jax
import jax.numpy as jnp
import numpy as np
from jax import lax
from jax.experimental import pallas as pl
from jax.experimental.pallas import tpu as pltpu
from jax.sharding import Mesh, PartitionSpec as P

HEADS = 8
HEAD_DIM = 88
SCALE = 1.0 / np.sqrt(np.float32(HEAD_DIM))
F32 = jnp.float32
BF16 = jnp.bfloat16
HIGH = lax.Precision.HIGH
AXES = ("z", "yh", "core", "yl", "x")
CTX = ("yl", "x")
FLIPS = ((3, 1), (1, 3))
PAIR = [(0, 1), (1, 0)]


def split(a):
    hi = a.astype(BF16)
    return hi, (a - hi.astype(F32)).astype(BF16)


def halves(a):
    hi = a.astype(BF16).astype(F32)
    return hi, a - hi


def padded(pieces, rows):
    used = sum(p.shape[0] for p in pieces)
    if used < rows:
        pieces = pieces + [jnp.zeros((rows - used, pieces[0].shape[1]), F32)]
    return jnp.concatenate(pieces, axis=0)


def attention_kernel(*refs):
    ins, outs, scratch = refs[:8], refs[8:14], refs[14:]
    packed, held, made, rk, rv, kc, vc, s_ref, ph_ref, pl_ref, dk, dv = scratch
    own, m1, m2, c10, c11, c13 = outs
    d = HEAD_DIM
    n = ins[0].shape[2]
    live_row = 4 * d
    dot = functools.partial(jnp.dot, preferred_element_type=F32)

    offset = [0]
    for block in ins:
        count = jnp.sum(block[0, live_row : live_row + 1]).astype(jnp.int32)
        offset.append(pl.multiple_of(offset[-1] + ((count + 7) & ~7), 8))
    for block, at in zip(ins, offset):
        packed[pl.ds(at, n), :] = padded([block[0]], packed.shape[1]).T
    packed[pl.ds(offset[-1], n), :] = jnp.zeros((n, packed.shape[1]), F32)
    used = (offset[-1] + n - 1) // n

    def at(b):
        return pl.ds(pl.multiple_of(b * n, n), n)

    def prepare(b, c):
        r = packed[at(b), :].T
        held[b] = r
        kh, kl = halves(r[d : 2 * d])
        vh, vl = halves(r[2 * d : 3 * d])
        below = lax.broadcasted_iota(jnp.int32, (8, n), 0) == 0
        dead = jnp.where(below, (r[live_row : live_row + 8] - 1.0) * 1e30, 0.0)
        rk[:, at(b)] = padded([kh, kh, kl, dead], rk.shape[0]).astype(BF16)
        rv[:, at(b)] = padded([vh, vh, vl], rv.shape[0]).astype(BF16)
        kc[at(b), :] = padded([kh, kl], 256).T.astype(BF16)
        vc[at(b), :] = padded([vh, vl], 256).T.astype(BF16)
        return c

    lax.fori_loop(0, used, prepare, 0)
    dk[...] = jnp.zeros_like(dk)
    dv[...] = jnp.zeros_like(dv)

    def queries(blocks, j):
        loop = functools.partial(
            lax.fori_loop, 0, blocks, **({"unroll": True} if isinstance(blocks, int) else {})
        )
        qh, ql = halves(held[j, 0:d] * SCALE)
        lq = padded([qh, ql, qh, jnp.ones((8, n), F32)], 384).T.astype(BF16)
        q2 = jnp.concatenate([qh, ql], axis=0).astype(BF16)

        def scores(b, m):
            s = dot(lq, rk[:, at(b)])
            s_ref[b] = s
            return jnp.maximum(m, jnp.maximum(s[:, :128], s[:, 128:]))

        m = loop(scores, jnp.full((n, 128), -1e30, F32))
        m = jnp.max(m, axis=1, keepdims=True)

        def probs(b, c):
            l, o = c
            p = jnp.exp(s_ref[b] - m)
            s_ref[b] = p
            ph, plo = split(p)
            ph_ref[b] = ph
            pl_ref[b] = plo
            v = vc[at(b), :]
            return l + (p[:, :128] + p[:, 128:]), o + (dot(ph, v) + dot(plo, v))

        l, o = loop(probs, (jnp.zeros((n, 128), F32), jnp.zeros((n, 256), F32)))
        rl = 1.0 / jnp.sum(l, axis=1, keepdims=True)
        o_t = (o * rl).T
        o_t = o_t[0:d] + o_t[d : 2 * d]
        made[j, 0:d] = o_t
        g_t = held[j, 3 * d : 4 * d] * jnp.broadcast_to(rl, (n, 128)).T[0:1]
        row_dot = jnp.sum(padded([g_t * o_t], 128).T, axis=1, keepdims=True)
        gh, gl = halves(g_t)
        lg = padded([gh, gl, gh], 384).T.astype(BF16)
        g2 = jnp.concatenate([gh, gl], axis=0).astype(BF16)

        def back(b, dq):
            dp = dot(lg, rv[:, at(b)])
            dh, dl = split(s_ref[b] * (dp - row_dot))
            k = kc[at(b), :]
            dv[:, at(b)] += dot(g2, ph_ref[b]) + dot(g2, pl_ref[b])
            dk[:, at(b)] += dot(q2, dh) + dot(q2, dl)
            return dq + (dot(dh, k) + dot(dl, k))

        dq = loop(back, jnp.zeros((n, 256), F32)).T
        made[j, d : 2 * d] = (dq[0:d] + dq[d : 2 * d]) * SCALE

    def all_queries(blocks):
        def body(j, c):
            queries(blocks, j)
            return c

        lax.fori_loop(0, blocks, body, 0)

    for blocks in (8, 7, 6, 5):
        pl.when(used == blocks)(functools.partial(all_queries, blocks))
    pl.when(used < 5)(functools.partial(all_queries, used))

    def finish(b, c):
        a = dk[:, at(b)]
        made[b, 2 * d : 3 * d] = a[0:d] + a[d : 2 * d]
        a = dv[:, at(b)]
        made[b, 3 * d : 4 * d] = a[0:d] + a[d : 2 * d]
        packed[at(b), :] = made[b].T
        return c

    lax.fori_loop(0, used, finish, 0)
    places = [(own, 0), (m1, 0), (m1, 1), (m2, 0), (c10, 0), (c11, 0), (m2, 1), (c13, 0)]
    for block, first, (out, i) in zip(ins, offset, places):
        rows = packed[pl.ds(first, n), :].T
        live = block[0, live_row : live_row + 1] > 0
        out[i] = jnp.where(live, rows[0 : 4 * d], 0.0)


def attention(blocks):
    rows, n = blocks[0].shape[1:]
    d = HEAD_DIM
    total = 8 * n
    first = lambda a: pl.BlockSpec((1, rows, n), lambda i: (0, 0, 0))
    counts = (1, 2, 2, 1, 1, 1)
    return pl.pallas_call(
        attention_kernel,
        grid=(1,),
        out_shape=[jax.ShapeDtypeStruct((c, 4 * d, n), F32) for c in counts],
        in_specs=[first(b) for b in blocks],
        out_specs=[pl.BlockSpec((c, 4 * d, n), lambda i: (0, 0, 0)) for c in counts],
        scratch_shapes=[
            pltpu.VMEM((total + n, 384), F32),
            pltpu.VMEM((8, 384, n), F32),
            pltpu.VMEM((8, 384, n), F32),
            pltpu.VMEM((384, total), BF16),
            pltpu.VMEM((384, total), BF16),
            pltpu.VMEM((total, 256), BF16),
            pltpu.VMEM((total, 256), BF16),
            pltpu.VMEM((8, n, n), F32),
            pltpu.VMEM((8, n, n), BF16),
            pltpu.VMEM((8, n, n), BF16),
            pltpu.VMEM((2 * d, total), F32),
            pltpu.VMEM((2 * d, total), F32),
        ],
        compiler_params=pltpu.CompilerParams(vmem_limit_bytes=52 * 2**20),
        name="attention",
    )(*blocks)


PART_TILES = (8, 7, 7)
PART_ROWS = (88, 80, 80)
PART_RINGS = ((2, 1, 0), (1, 0, 2), (0, 2, 1))


def weights_kernel(where, near, far, *refs):
    own, other, refs = refs[:8], refs[8:16], refs[16:]
    sends, keeps, (n3, m3, g3, a3, w, grads) = refs[:3], refs[3:6], refs[6:]
    d = HEAD_DIM
    half = near.shape[3]
    rows = near.shape[1] * d
    wide = HEADS * d
    z, yh, core, yl, x = [where[i] for i in range(5)]

    def keep(at, to, lo, pieces):
        for i, p in enumerate(pieces):
            h, l = split(p)
            for k in range(3):
                to[at, (2 * k + i) * half : (2 * k + i + 1) * half] = (h, l)[k == lo]

    keep(slice(0, rows), n3, 2, [r[0].reshape(rows, half) for r in (near, far)])
    keep(slice(0, rows), m3, 2, [r[1].reshape(rows, half) for r in (near, far)])
    for i, blocks in enumerate((own, other)):
        for p, block in enumerate(blocks):
            grads[(yl * 4 + x) ^ p, :, i * half : (i + 1) * half] = block[0]
    for pair in range(HEADS // 2):
        for kind in range(4):
            pieces = [
                jnp.concatenate(
                    [
                        grads[2 * pair + k, kind * d : (kind + 1) * d, i * half : (i + 1) * half]
                        for k in range(2)
                    ],
                    axis=0,
                )
                for i in range(2)
            ]
            first = ((kind - 1) * wide if kind else 0) + 2 * pair * d
            keep(slice(first, first + 2 * d), g3 if kind else a3, 1, pieces)
    dot = functools.partial(
        lax.dot_general,
        dimension_numbers=(((1,), (1,)), ((), ())),
        preferred_element_type=F32,
    )
    for first in range(0, 3 * wide, 768):
        last = min(first + 768, 3 * wide)
        w[:, first:last] = dot(n3[...], g3[first:last, :])
    w[:, 3 * wide :] = dot(m3[...], a3[...])

    for refs in (sends, keeps):
        for ref in refs[1:]:
            ref[:, :, :, 72:80, :] = jnp.zeros((2, 2, 8, 8, 128), F32)

    def bits(p):
        mixed = (p ^ (p >> 1)) & 1
        first = jnp.where(core == 0, p >> 1, mixed)
        return first, jnp.where(core == 0, mixed, p >> 1)

    def scatter(zy, carry):
        at = pl.ds(pl.multiple_of(zy * d, 8), d)
        z_bits = bits(z ^ (zy >> 1))
        for c in range(8):
            y_bits = bits(((yh ^ (zy & 1)) << 1) | (yl ^ (c >> 2)))
            x_bits = bits(x ^ (c & 3))
            a = (z_bits[0], y_bits[0], x_bits[0])
            j = (z_bits[1] << 2) | (y_bits[1] << 1) | x_bits[1]
            tile = 0
            for part in range(3):
                r0, r1, r2 = PART_RINGS[part]

                def store(ref, tile=tile, part=part, r1=r1, r2=r2, a=a, j=j, c=c):
                    for t in range(PART_TILES[part]):
                        block = w[at, (tile + t) * 128 : (tile + t + 1) * 128]
                        ref[a[r1], a[r2], j, t * 11 : (t + 1) * 11, :] = block[c * 11 : (c + 1) * 11]

                pl.when(a[r0] == 1)(functools.partial(store, sends[part]))
                pl.when(a[r0] == 0)(functools.partial(store, keeps[part]))
                tile += PART_TILES[part]
        return carry

    lax.fori_loop(0, 8, scatter, 0)


def weight_grads(where, *arrays):
    _, blocks, _, half = arrays[0].shape
    rows = blocks * HEAD_DIM
    wide = HEADS * HEAD_DIM
    vmem = pl.BlockSpec(memory_space=pltpu.VMEM)
    return pl.pallas_call(
        weights_kernel,
        in_specs=[pl.BlockSpec(memory_space=pltpu.SMEM)] + [vmem] * len(arrays),
        out_specs=[vmem] * 6,
        out_shape=[jax.ShapeDtypeStruct((2, 2, 8, r, 128), F32) for r in PART_ROWS] * 2,
        scratch_shapes=[
            pltpu.VMEM((rows, 6 * half), BF16),
            pltpu.VMEM((rows, 6 * half), BF16),
            pltpu.VMEM((3 * wide, 6 * half), BF16),
            pltpu.VMEM((wide, 6 * half), BF16),
            pltpu.VMEM((rows, 4 * wide), F32),
            pltpu.VMEM((HEADS, 4 * HEAD_DIM, 2 * half), F32),
        ],
        compiler_params=pltpu.CompilerParams(vmem_limit_bytes=56 * 2**20),
        name="weight_grads",
    )(where, *arrays)


def index_of(z, y, core, x):
    return (((z * 2 + (y >> 1)) * 2 + core) * 2 + (y & 1)) * 4 + x


def swap_over(piece, flips, which):
    pairs = []
    for z in range(4):
        for y in range(4):
            for core in range(2):
                f = FLIPS[core][which]
                for x in range(4):
                    to = index_of(z ^ (f * flips[0]), y ^ (f * flips[1]), core, x ^ (f * flips[2]))
                    pairs.append((index_of(z, y, core, x), to))
    return lax.ppermute(piece, AXES, pairs)


def sum_over_chips(sends, keeps, beside):
    flips = lambda r: [int(r == k) for k in range(3)]
    sent = lax.optimization_barrier(list(sends))
    got = [swap_over(s, flips(r[0]), 0) for s, r in zip(sent, PART_RINGS)]
    got, beside = lax.optimization_barrier((got, beside))
    kept = list(keeps)
    for step in (1, 2):
        sent = lax.optimization_barrier([k[1] + g[1] for k, g in zip(kept, got)])
        kept = [k[0] + g[0] for k, g in zip(kept, got)]
        got = [swap_over(s, flips(r[step]), 0) for s, r in zip(sent, PART_RINGS)]
        got = lax.optimization_barrier(got)
    rest = jnp.concatenate([k + g for k, g in zip(kept, got)], axis=1)
    rest = rest.reshape(4, 2, *rest.shape[1:])
    sent = lax.optimization_barrier([rest[1], rest[2], rest[3]])
    got = [swap_over(s, f, 1) for s, f in zip(sent, ((0, 1, 0), (1, 0, 0), (1, 1, 0)))]
    rest = sum(lax.optimization_barrier(got), rest[0])
    return rest[0] + swap_over(rest[1], (0, 0, 1), 1), beside


def exchange(messages):
    own, m1, m2, c10, c11, c13 = messages
    send = lambda a, p: lax.ppermute(a, CTX, [(i, i ^ p) for i in range(8)])
    m1, m2, c11, c13, c10 = lax.optimization_barrier((m1, m2, c11, c13, c10))
    got = [send(m1, 1), send(m2, 3), send(c10, 4), send(c11, 5), send(c13, 7)]
    g1, g2, r10, r11, r13 = lax.optimization_barrier(got)
    return [own, g1, send(g1[1:2], 3), g2, r10, r11, send(g2[1:2], 5), r13]


def other_core(a):
    return lax.ppermute(a, "core", PAIR)


def layer_norm(x):
    centred = x - jnp.sum(x, axis=1, keepdims=True) / x.shape[1]
    var = jnp.sum(centred * centred, axis=1, keepdims=True) / x.shape[1]
    inv_std = lax.rsqrt(var + 1e-06)
    return centred * inv_std, inv_std


def masked_rows(ref, count):
    rows = lax.broadcasted_iota(jnp.int32, ref.shape, 0)
    return jnp.where(rows < count[0, 0], ref[...], 0.0)


def dot_rows(a, b):
    return lax.dot_general(a, b, (((1,), (1,)), ((), ())), preferred_element_type=F32)


def front_kernel(where, count, x_ref, c_ref, w_ref, o_ref, *refs):
    messages, (near, far), (n2, turned) = refs[:6], refs[6:8], refs[8:]
    d = HEAD_DIM
    wide = HEADS * d
    slots = x_ref.shape[0]
    step = pl.program_id(0)

    def project(w, hi, lo):
        wh, wl = split(w)
        return dot_rows(wh, hi) + (dot_rows(wl, hi) + dot_rows(wh, lo))

    @pl.when(step == 0)
    def _():
        normed, _ = layer_norm(x_ref[...])
        n2[0:slots, :], n2[slots:, :] = split(normed)
        masked = masked_rows(c_ref, count)
        core = where[2]
        for k, a in enumerate((normed, masked)):
            turned[0 : a.shape[1], :] = a.T
            for i in range(8):
                for ref, c in ((near, core), (far, 1 - core)):
                    ref[k, i] = turned[pl.ds(pl.multiple_of((2 * i + c) * d, 8), d), :]
        turned[3 * wide :, :] = project(o_ref[...], *split(masked))

    turned[pl.ds(pl.multiple_of(step * wide, 8), wide), :] = project(
        w_ref[...], n2[0:slots, :], n2[slots:, :]
    )

    @pl.when(step == pl.num_programs(0) - 1)
    def _():
        lanes = lax.broadcasted_iota(jnp.int32, (8, slots), 1)
        valid = (lanes < count[0, 0]).astype(F32)
        for p, (i, k) in enumerate(MESSAGE_OF):
            head = (where[3] * 4 + where[4]) ^ p
            for kind in range(4):
                at = pl.ds(pl.multiple_of(head * d + kind * wide, 8), d)
                messages[i][k, kind * d : (kind + 1) * d, :] = turned[at, :]
            messages[i][k, 4 * d :, :] = valid


MESSAGE_OF = ((0, 0), (1, 0), (1, 1), (2, 0), (3, 0), (4, 0), (2, 1), (5, 0))
MESSAGE_BLOCKS = (1, 2, 2, 1, 1, 1)


def whole(a):
    return pl.BlockSpec(a.shape, lambda i: (0,) * len(a.shape))


def front(where, count, x, c, w_t, w_out):
    slots, width = x.shape
    smem = pl.BlockSpec(memory_space=pltpu.SMEM)
    step = w_t.shape[0] // 3
    outs = [jax.ShapeDtypeStruct((b, 4 * HEAD_DIM + 8, slots), F32) for b in MESSAGE_BLOCKS]
    outs += [jax.ShapeDtypeStruct((2, 8, HEAD_DIM, slots), F32)] * 2
    return pl.pallas_call(
        front_kernel,
        grid=(3,),
        in_specs=[smem, smem, whole(x), whole(c), pl.BlockSpec((step, width), lambda i: (i, 0)), whole(w_out)],
        out_specs=[whole(a) for a in outs],
        out_shape=outs,
        scratch_shapes=[
            pltpu.VMEM((2 * slots, width), BF16),
            pltpu.VMEM((4 * HEADS * HEAD_DIM, slots), F32),
        ],
        compiler_params=pltpu.CompilerParams(vmem_limit_bytes=56 * 2**20),
        name="front",
    )(where, count, x, c, w_t, w_out)


def finish_kernel(where, count, x_ref, c_ref, *refs):
    blocks, (w_ref, o_ref, mixed, grad, g2, acc, turned) = refs[:8], refs[8:]
    d = HEAD_DIM
    wide = HEADS * d
    slots, width = x_ref.shape
    step = pl.program_id(0)

    @pl.when(step == 0)
    def _():
        for p, block in enumerate(blocks):
            head = (where[3] * 4 + where[4]) ^ p
            for kind in range(4):
                at = pl.ds(pl.multiple_of(head * d + kind * wide, 8), d)
                turned[at, :] = block[0, kind * d : (kind + 1) * d]
        g2[0:slots, :], g2[slots:, :] = split(turned[wide:, :].T)
        ah, al = split(turned[0:wide, :].T)
        oh, ol = split(o_ref[...])
        r = jnp.dot(jnp.concatenate([ah, al], axis=0), oh, preferred_element_type=F32)
        r2 = jnp.dot(ah, ol, preferred_element_type=F32)
        rows = lax.broadcasted_iota(jnp.int32, x_ref.shape, 0)
        projected = r[0:slots] + (r[slots:] + r2)
        mixed[...] = jnp.where(rows < count[0, 0], x_ref[...] + projected, 0.0)

    wh, wl = split(w_ref[...])
    r = jnp.dot(g2[...], wh, preferred_element_type=F32)
    r2 = jnp.dot(g2[0:slots, :], wl, preferred_element_type=F32)
    acc[step] = r[0:slots] + (r[slots:] + r2)

    @pl.when(step == pl.num_programs(0) - 1)
    def _():
        g = jnp.concatenate([acc[i] for i in range(acc.shape[0])], axis=1)[:, 0:width]
        normed, inv_std = layer_norm(x_ref[...])
        mean = jnp.sum(g, axis=1, keepdims=True) / width
        along = jnp.sum(g * normed, axis=1, keepdims=True) / width
        grad[...] = masked_rows(c_ref, count) + inv_std * (g - mean - normed * along)


def finish(where, count, x, c, blocks, w_t, w_out):
    slots, width = x.shape
    smem = pl.BlockSpec(memory_space=pltpu.SMEM)
    step = 512
    steps = -(-width // step)
    columns = w_t.shape[0]
    first = lambda a: pl.BlockSpec((1,) + a.shape[1:], lambda i: (0, 0, 0))
    return pl.pallas_call(
        finish_kernel,
        grid=(steps,),
        in_specs=[smem, smem, whole(x), whole(c)]
        + [first(b) for b in blocks]
        + [pl.BlockSpec((columns, step), lambda i: (0, i)), whole(w_out)],
        out_specs=[whole(x), whole(x)],
        out_shape=[jax.ShapeDtypeStruct(x.shape, F32)] * 2,
        scratch_shapes=[
            pltpu.VMEM((2 * slots, columns), BF16),
            pltpu.VMEM((steps, slots, step), F32),
            pltpu.VMEM((4 * HEADS * HEAD_DIM, slots), F32),
        ],
        compiler_params=pltpu.CompilerParams(vmem_limit_bytes=56 * 2**20),
        cost_estimate=pl.CostEstimate(flops=10**10, bytes_accessed=25 * 10**6, transcendentals=0),
        name="finish",
    )(where, count, x, c, *blocks, w_t, w_out)


def per_device(tokens, counts, w_qkv, w_out, cotangent):
    where = jnp.stack([lax.axis_index(a) for a in AXES]).astype(jnp.int32)
    x, c = tokens[0], cotangent[0]
    w_t = w_qkv.T
    *messages, near, far = front(where, counts, x, c, w_t, w_out)
    blocks = exchange(messages)
    blocks, far = lax.optimization_barrier((blocks, far))
    far = other_core(far)
    back = exchange(attention(blocks))
    others = [other_core(b) for b in back]
    sums = weight_grads(where, near, far, *back, *others)
    back, sums = lax.optimization_barrier((back, sums))
    outs = finish(where, counts, x, c, back, w_t, w_out)
    share, (mixed, grad_tokens) = sum_over_chips(sums[:3], sums[3:], outs)

    share = jnp.concatenate([share[: 15 * 11], share[168 : 168 + 7 * 11]], axis=0)
    share = share.reshape(22, 11, 128).transpose(1, 0, 2).reshape(11, 22 * 128)
    wide = 3 * HEADS * HEAD_DIM
    return (mixed[None], grad_tokens[None], share[:, :wide], share[:, wide:].T)


def solution(mesh):
    split_mesh = Mesh(mesh.devices.reshape(4, 2, 2, 2, 4), AXES)
    dp, ctx = ("z", "yh", "core"), CTX
    return jax.shard_map(
        per_device,
        mesh=split_mesh,
        in_specs=(P(dp, ctx, None), P(dp, ctx), P(), P(), P(dp, ctx, None)),
        out_specs=(
            P(dp, ctx, None),
            P(dp, ctx, None),
            P(dp + ctx, None),
            P(None, dp + ctx),
        ),
        check_vma=False,
    )
```

```python
import functools

import jax
import jax.numpy as jnp
import numpy as np
from jax import lax
from jax.experimental import pallas as pl
from jax.experimental.pallas import tpu as pltpu
from jax.sharding import Mesh, PartitionSpec as P

HEADS = 8
HEAD_DIM = 88
SCALE = 1.0 / np.sqrt(np.float32(HEAD_DIM))
F32 = jnp.float32
BF16 = jnp.bfloat16
HIGH = lax.Precision.HIGH
AXES = ("z", "yh", "core", "yl", "x")
CTX = ("yl", "x")
FLIPS = ((3, 1), (1, 3))
PAIR = [(0, 1), (1, 0)]


def split(a):
    hi = a.astype(BF16)
    return hi, (a - hi.astype(F32)).astype(BF16)


def halves(a):
    hi = a.astype(BF16).astype(F32)
    return hi, a - hi


LEAST = 5
LANES = 128


def attention_kernel(*refs):
    ins, outs, scratch = refs[:8], refs[8:16], refs[16:]
    packed, rk, rv, kc, vc, s_ref, pp, ds, dk, dv = scratch
    d = HEAD_DIM
    n = ins[0].shape[2]
    live_row = 4 * d
    dot = functools.partial(jnp.dot, preferred_element_type=F32)
    group = lambda i: slice(i * LANES, (i + 1) * LANES)

    offset = [0]
    for block in ins:
        count = jnp.sum(block[0, live_row : live_row + 1]).astype(jnp.int32)
        offset.append(pl.multiple_of(offset[-1] + ((count + 7) & ~7), 8))
    top = lax.broadcasted_iota(jnp.int32, (8, n), 0) == 0
    zeros = lambda rows: jnp.zeros((rows, n), F32)
    for block, first in zip(ins, offset):
        r = block[0]
        one = jnp.where(top, 1.0, 0.0)
        dead = jnp.where(top, (r[live_row:] - 1.0) * 1e30, 0.0)
        pieces = [r[0:d], one, zeros(32), r[3 * d : 4 * d], zeros(40)]
        pieces += [r[d : 2 * d], dead, zeros(32), r[2 * d : 3 * d], zeros(40)]
        packed[pl.ds(first, n), :] = jnp.concatenate(pieces, axis=0).T
    lanes = lax.broadcasted_iota(jnp.int32, (n, 4 * LANES), 1)
    nothing = jnp.where(lanes == 2 * LANES + d, -1e30, 0.0)
    packed[pl.ds(offset[-1], n), :] = nothing
    used = jnp.maximum((offset[-1] + n - 1) // n, LEAST)
    for b in range(LEAST):

        @pl.when(offset[-1] <= b * n)
        def _(b=b):
            packed[b * n : (b + 1) * n, :] = nothing

    def at(b):
        return pl.ds(pl.multiple_of(b * n, n), n)

    def prepare(b, c):
        t = packed[at(b), 2 * LANES :].T
        for i, (wide, rows) in enumerate(((rk, kc), (rv, vc))):
            hi, lo = split(t[group(i)])
            wide[group(0), at(b)] = hi
            wide[group(1), at(b)] = hi
            wide[group(2), at(b)] = lo
            rows[at(b), group(0)], rows[at(b), group(1)] = split(packed[at(b), group(2 + i)])
        return c

    lax.fori_loop(0, used, prepare, 0)
    dk[...] = jnp.zeros_like(dk)
    dv[...] = jnp.zeros_like(dv)

    def stacked(a):
        hi, lo = halves(a.T)
        both = jnp.concatenate([hi[0:d], lo[0:d]], axis=0).astype(BF16)
        return jnp.concatenate([both, both], axis=1)

    def fold(a):
        a = a[0:n] + a[n:]
        return a[:, group(0)] + a[:, group(1)]

    def queries(blocks, j):
        keys = blocks * n
        cuts = (0, keys) if blocks != 7 else (0, keys - n, keys)
        spans = [slice(a, b) for a, b in zip(cuts, cuts[1:])]
        tiles = [slice(b * n, (b + 1) * n) for b in range(blocks)]
        q = packed[at(j), group(0)] * SCALE
        qh, ql = split(q)
        lq = jnp.concatenate([qh, ql, qh], axis=1)
        m = jnp.full((n, LANES), -1e30, F32)
        for t in tiles:
            s = dot(lq, rk[:, t])
            s_ref[:, t] = s
            m = jnp.maximum(m, jnp.maximum(s[:, group(0)], s[:, group(1)]))
        m = jnp.max(m, axis=1, keepdims=True)
        l = jnp.zeros((n, LANES), F32)
        for t in tiles:
            p = jnp.exp(s_ref[:, t] - m)
            s_ref[:, t] = p
            pp[0:n, t], pp[n:, t] = split(p)
            l = l + (p[:, group(0)] + p[:, group(1)])
        o = sum(dot(pp[:, s], vc[s, :]) for s in spans)
        rl = 1.0 / jnp.sum(l, axis=1, keepdims=True)
        o = fold(o) * rl
        g = packed[at(j), group(1)] * rl
        row_dot = jnp.sum(g * o, axis=1, keepdims=True)
        gh, gl = split(g)
        lg = jnp.concatenate([gh, gl, gh], axis=1)
        g2 = stacked(g)
        for s in spans:
            dv[:, s] += dot(g2, pp[:, s])
        for t in tiles:
            grad = s_ref[:, t] * (dot(lg, rv[:, t]) - row_dot)
            ds[0:n, t], ds[n:, t] = split(grad)
        q2 = stacked(q)
        for s in spans:
            dk[:, s] += dot(q2, ds[:, s])
        packed[at(j), group(0)] = o
        packed[at(j), group(1)] = fold(sum(dot(ds[:, s], kc[s, :]) for s in spans)) * SCALE

    def all_queries(blocks):
        def body(j, c):
            queries(blocks, j)
            return c

        lax.fori_loop(0, blocks, body, 0)

    for blocks in range(LEAST, 9):
        pl.when(used == blocks)(functools.partial(all_queries, blocks))

    def finish_keys(b, c):
        for i, ref in enumerate((dk, dv)):
            a = ref[:, at(b)]
            a = jnp.concatenate([a[0:d] + a[d:], zeros(40)], axis=0)
            packed[at(b), group(2 + i)] = a.T
        return c

    lax.fori_loop(0, used, finish_keys, 0)
    for block, first, out in zip(ins, offset, outs):
        rows = packed[pl.ds(first, n), :].T
        live = block[0, live_row : live_row + 1] > 0
        for k in range(4):
            out[0, k * d : (k + 1) * d] = jnp.where(live, rows[k * LANES : k * LANES + d], 0.0)


def attention(blocks):
    rows, n = blocks[0].shape[1:]
    d = HEAD_DIM
    total = 8 * n
    first = lambda a: pl.BlockSpec((1, rows, n), lambda i: (0, 0, 0))
    return pl.pallas_call(
        attention_kernel,
        grid=(1,),
        out_shape=[jax.ShapeDtypeStruct((1, 4 * d, n), F32)] * 8,
        in_specs=[first(b) for b in blocks],
        out_specs=[pl.BlockSpec((1, 4 * d, n), lambda i: (0, 0, 0))] * 8,
        scratch_shapes=[
            pltpu.VMEM((total + n, 4 * LANES), F32),
            pltpu.VMEM((3 * LANES, total), BF16),
            pltpu.VMEM((3 * LANES, total), BF16),
            pltpu.VMEM((total, 2 * LANES), BF16),
            pltpu.VMEM((total, 2 * LANES), BF16),
            pltpu.VMEM((n, total), F32),
            pltpu.VMEM((2 * n, total), BF16),
            pltpu.VMEM((2 * n, total), BF16),
            pltpu.VMEM((2 * d, total), F32),
            pltpu.VMEM((2 * d, total), F32),
        ],
        compiler_params=pltpu.CompilerParams(vmem_limit_bytes=52 * 2**20),
        name="attention",
    )(*blocks)


PART_TILES = (8, 7, 7)
PART_ROWS = (88, 80, 80)
PART_RINGS = ((2, 1, 0), (1, 0, 2), (0, 2, 1))


def weights_kernel(where, near, far, *refs):
    own, other, refs = refs[:8], refs[8:16], refs[16:]
    sends, keeps, (n3, m3, g3, a3, w, grads) = refs[:3], refs[3:6], refs[6:]
    d = HEAD_DIM
    half = near.shape[3]
    rows = near.shape[1] * d
    wide = HEADS * d
    z, yh, core, yl, x = [where[i] for i in range(5)]

    def keep(at, to, lo, pieces):
        for i, p in enumerate(pieces):
            h, l = split(p)
            for k in range(3):
                to[at, (2 * k + i) * half : (2 * k + i + 1) * half] = (h, l)[k == lo]

    keep(slice(0, rows), n3, 2, [r[0].reshape(rows, half) for r in (near, far)])
    keep(slice(0, rows), m3, 2, [r[1].reshape(rows, half) for r in (near, far)])
    for i, blocks in enumerate((own, other)):
        for p, block in enumerate(blocks):
            grads[(yl * 4 + x) ^ p, :, i * half : (i + 1) * half] = block[0]
    for pair in range(HEADS // 2):
        for kind in range(4):
            pieces = [
                jnp.concatenate(
                    [
                        grads[2 * pair + k, kind * d : (kind + 1) * d, i * half : (i + 1) * half]
                        for k in range(2)
                    ],
                    axis=0,
                )
                for i in range(2)
            ]
            first = ((kind - 1) * wide if kind else 0) + 2 * pair * d
            keep(slice(first, first + 2 * d), g3 if kind else a3, 1, pieces)
    dot = functools.partial(
        lax.dot_general,
        dimension_numbers=(((1,), (1,)), ((), ())),
        preferred_element_type=F32,
    )
    for first in range(0, 3 * wide, 768):
        last = min(first + 768, 3 * wide)
        w[:, first:last] = dot(n3[...], g3[first:last, :])
    w[:, 3 * wide :] = dot(m3[...], a3[...])

    for refs in (sends, keeps):
        for ref in refs[1:]:
            ref[:, :, :, 72:80, :] = jnp.zeros((2, 2, 8, 8, 128), F32)

    def bits(own, to):
        p = own ^ to
        first = jnp.where(core == 0, p >> 1, (p ^ (p >> 1)) & 1)
        return first, jnp.where(core == 0, to & 1, to >> 1)

    def scatter(zy, carry):
        at = pl.ds(pl.multiple_of(zy * d, 8), d)
        z_bits = bits(z, zy >> 1)
        for c in range(8):
            y_bits = bits((yh << 1) | yl, ((zy & 1) << 1) | (c >> 2))
            x_bits = bits(x, c & 3)
            a = (z_bits[0], y_bits[0], x_bits[0])
            j = (z_bits[1] << 2) | (y_bits[1] << 1) | x_bits[1]
            tile = 0
            for part in range(3):
                r0, r1, r2 = PART_RINGS[part]

                def store(ref, tile=tile, part=part, r1=r1, r2=r2, a=a, j=j, c=c):
                    for t in range(PART_TILES[part]):
                        block = w[at, (tile + t) * 128 : (tile + t + 1) * 128]
                        ref[a[r1], a[r2], j, t * 11 : (t + 1) * 11, :] = block[c * 11 : (c + 1) * 11]

                pl.when(a[r0] == 1)(functools.partial(store, sends[part]))
                pl.when(a[r0] == 0)(functools.partial(store, keeps[part]))
                tile += PART_TILES[part]
        return carry

    lax.fori_loop(0, 8, scatter, 0)


def weight_grads(where, *arrays):
    _, blocks, _, half = arrays[0].shape
    rows = blocks * HEAD_DIM
    wide = HEADS * HEAD_DIM
    vmem = pl.BlockSpec(memory_space=pltpu.VMEM)
    return pl.pallas_call(
        weights_kernel,
        in_specs=[pl.BlockSpec(memory_space=pltpu.SMEM)] + [vmem] * len(arrays),
        out_specs=[vmem] * 6,
        out_shape=[jax.ShapeDtypeStruct((2, 2, 8, r, 128), F32) for r in PART_ROWS] * 2,
        scratch_shapes=[
            pltpu.VMEM((rows, 6 * half), BF16),
            pltpu.VMEM((rows, 6 * half), BF16),
            pltpu.VMEM((3 * wide, 6 * half), BF16),
            pltpu.VMEM((wide, 6 * half), BF16),
            pltpu.VMEM((rows, 4 * wide), F32),
            pltpu.VMEM((HEADS, 4 * HEAD_DIM, 2 * half), F32),
        ],
        compiler_params=pltpu.CompilerParams(vmem_limit_bytes=56 * 2**20),
        name="weight_grads",
    )(where, *arrays)


def index_of(z, y, core, x):
    return (((z * 2 + (y >> 1)) * 2 + core) * 2 + (y & 1)) * 4 + x


def swap_over(piece, flips, which):
    pairs = []
    for z in range(4):
        for y in range(4):
            for core in range(2):
                f = FLIPS[core][which]
                for x in range(4):
                    to = index_of(z ^ (f * flips[0]), y ^ (f * flips[1]), core, x ^ (f * flips[2]))
                    pairs.append((index_of(z, y, core, x), to))
    return lax.ppermute(piece, AXES, pairs)


def sum_over_chips(sends, keeps, beside):
    flips = lambda r: [int(r == k) for k in range(3)]
    sent = lax.optimization_barrier(list(sends))
    got = [swap_over(s, flips(r[0]), 0) for s, r in zip(sent, PART_RINGS)]
    got, beside = lax.optimization_barrier((got, beside))
    kept = list(keeps)
    for step in (1, 2):
        sent = lax.optimization_barrier([k[1] + g[1] for k, g in zip(kept, got)])
        kept = [k[0] + g[0] for k, g in zip(kept, got)]
        got = [swap_over(s, flips(r[step]), 0) for s, r in zip(sent, PART_RINGS)]
        got = lax.optimization_barrier(got)
    rest = jnp.concatenate([k + g for k, g in zip(kept, got)], axis=1)
    got = lax.all_to_all(rest, AXES, 0, 0, axis_index_groups=last_groups(), tiled=True)
    return jnp.sum(got, axis=0), beside


def last_groups():
    groups = {}
    for z in range(4):
        for y in range(4):
            for core in range(2):
                for x in range(4):
                    kept = lambda i: (i ^ (i >> 1)) & 1 if core else i >> 1
                    label = lambda i: i >> 1 if core else i & 1
                    key = (core, kept(z), kept(y), kept(x))
                    groups.setdefault(key, []).append(((label(z), label(y), label(x)), index_of(z, y, core, x)))
    return [[i for _, i in sorted(g)] for g in groups.values()]


def exchange(early, late):
    send = lambda a, p: lax.ppermute(a, CTX, [(i, i ^ p) for i in range(8)])
    b2, b6, b5, b7 = early
    g2, g6, r5, r7 = send(b2, 1), send(b6, 3), send(b5, 5), send(b7, 7)
    g2, g6, late = lax.optimization_barrier((g2, g6, late))
    b0, b1, b3, b4 = late
    f2, f6 = send(g2, 3), send(g6, 5)
    return [b0, send(b1, 1), f2, send(b3, 3), send(b4, 4), r5, f6, r7]


def other_core(a):
    return lax.ppermute(a, "core", PAIR)


def layer_norm(x):
    centred = x - jnp.sum(x, axis=1, keepdims=True) / x.shape[1]
    var = jnp.sum(centred * centred, axis=1, keepdims=True) / x.shape[1]
    inv_std = lax.rsqrt(var + 1e-06)
    return centred * inv_std, inv_std


def masked_rows(ref, count):
    rows = lax.broadcasted_iota(jnp.int32, ref.shape, 0)
    return jnp.where(rows < count[0, 0], ref[...], 0.0)


def dot_rows(a, b):
    return lax.dot_general(a, b, (((1,), (1,)), ((), ())), preferred_element_type=F32)


EARLY = (2, 6, 5, 7)
LATE = (0, 1, 3, 4)


def whole(a):
    return pl.BlockSpec(a.shape, lambda *i: (0,) * len(a.shape))


def front_kernel(features, heads, where, count, x_ref, c_ref, q_ref, k_ref, v_ref, o_ref, *refs):
    messages, refs = refs[:4], refs[4:]
    nh, nl, mh, ml = refs[-4:]
    d = HEAD_DIM
    slots = x_ref.shape[0]
    step = pl.program_id(0)

    @pl.when(step == 0)
    def _():
        normed, _ = layer_norm(x_ref[...])
        masked = masked_rows(c_ref, count)
        nh[...], nl[...] = split(normed)
        mh[...], ml[...] = split(masked)
        if features:
            near, far, turned = refs[:3]
            core = where[2]
            for k, a in enumerate((normed, masked)):
                turned[...] = a.T
                for i in range(8):
                    for ref, c in ((near, core), (far, 1 - core)):
                        ref[k, i] = turned[pl.ds(pl.multiple_of((2 * i + c) * d, 8), d), :]

    def project(w, hi, lo):
        rows = w.shape[0]
        wh, wl = halves(w)
        both = dot_rows(jnp.concatenate([wh, wl], axis=0).astype(BF16), hi[...])
        return both[0:rows] + (both[rows:] + dot_rows(wh.astype(BF16), lo[...]))

    qkv = project(jnp.concatenate([q_ref[...], k_ref[...], v_ref[...]], axis=0), nh, nl)
    grads = project(o_ref[...], mh, ml)
    lanes = lax.broadcasted_iota(jnp.int32, (8, slots), 1)
    for i, message in enumerate(messages):

        @pl.when(step == i)
        def _(message=message):
            message[0, 0 : 3 * d, :] = qkv
            message[0, 3 * d : 4 * d, :] = grads
            message[0, 4 * d :, :] = (lanes < count[0, 0]).astype(F32)


def front(heads, where, count, x, c, w_t, w_out, features):
    slots, width = x.shape
    d = HEAD_DIM
    part = lambda kind: pl.BlockSpec((d, width), lambda i, h, *_: (kind * HEADS + h[i], 0))
    outs = [jax.ShapeDtypeStruct((1, 4 * d + 8, slots), F32)] * 4
    scratch = [pltpu.VMEM((slots, width), BF16)] * 4
    if features:
        outs += [jax.ShapeDtypeStruct((2, 8, d, slots), F32)] * 2
        scratch = [pltpu.VMEM((width, slots), F32)] + scratch
    return pl.pallas_call(
        functools.partial(front_kernel, features),
        grid_spec=pltpu.PrefetchScalarGridSpec(
            num_scalar_prefetch=3,
            grid=(4,),
            in_specs=[whole(x), whole(c), part(0), part(1), part(2), part(0)],
            out_specs=[whole(a) for a in outs],
            scratch_shapes=scratch,
        ),
        out_shape=outs,
        compiler_params=pltpu.CompilerParams(vmem_limit_bytes=58 * 2**20),
        cost_estimate=pl.CostEstimate(flops=6 * 10**9, bytes_accessed=14 * 10**6, transcendentals=0),
        name="front",
    )(heads, where, count, x, c, w_t, w_t, w_t, w_out)


def finish_kernel(where, count, x_ref, c_ref, *refs):
    blocks, (w_ref, o_ref, mixed, grad, g2, acc, turned) = refs[:8], refs[8:]
    d = HEAD_DIM
    wide = HEADS * d
    slots, width = x_ref.shape
    step = pl.program_id(0)

    @pl.when(step == 0)
    def _():
        for p, block in enumerate(blocks):
            head = (where[3] * 4 + where[4]) ^ p
            for kind in range(4):
                at = pl.ds(pl.multiple_of(head * d + kind * wide, 8), d)
                turned[at, :] = block[0, kind * d : (kind + 1) * d]
        g2[0:slots, :], g2[slots:, :] = split(turned[wide:, :].T)
        ah, al = split(turned[0:wide, :].T)
        oh, ol = split(o_ref[...])
        r = jnp.dot(jnp.concatenate([ah, al], axis=0), oh, preferred_element_type=F32)
        r2 = jnp.dot(ah, ol, preferred_element_type=F32)
        rows = lax.broadcasted_iota(jnp.int32, x_ref.shape, 0)
        projected = r[0:slots] + (r[slots:] + r2)
        mixed[...] = jnp.where(rows < count[0, 0], x_ref[...] + projected, 0.0)

    wh, wl = split(w_ref[...])
    r = jnp.dot(g2[...], wh, preferred_element_type=F32)
    r2 = jnp.dot(g2[0:slots, :], wl, preferred_element_type=F32)
    acc[step] = r[0:slots] + (r[slots:] + r2)

    @pl.when(step == pl.num_programs(0) - 1)
    def _():
        g = jnp.concatenate([acc[i] for i in range(acc.shape[0])], axis=1)[:, 0:width]
        normed, inv_std = layer_norm(x_ref[...])
        mean = jnp.sum(g, axis=1, keepdims=True) / width
        along = jnp.sum(g * normed, axis=1, keepdims=True) / width
        grad[...] = masked_rows(c_ref, count) + inv_std * (g - mean - normed * along)


def finish(where, count, x, c, blocks, w_t, w_out):
    slots, width = x.shape
    smem = pl.BlockSpec(memory_space=pltpu.SMEM)
    step = 512
    steps = -(-width // step)
    columns = w_t.shape[0]
    first = lambda a: pl.BlockSpec((1,) + a.shape[1:], lambda i: (0, 0, 0))
    return pl.pallas_call(
        finish_kernel,
        grid=(steps,),
        in_specs=[smem, smem, whole(x), whole(c)]
        + [first(b) for b in blocks]
        + [pl.BlockSpec((columns, step), lambda i: (0, i)), whole(w_out)],
        out_specs=[whole(x), whole(x)],
        out_shape=[jax.ShapeDtypeStruct(x.shape, F32)] * 2,
        scratch_shapes=[
            pltpu.VMEM((2 * slots, columns), BF16),
            pltpu.VMEM((steps, slots, step), F32),
            pltpu.VMEM((4 * HEADS * HEAD_DIM, slots), F32),
        ],
        compiler_params=pltpu.CompilerParams(vmem_limit_bytes=56 * 2**20),
        cost_estimate=pl.CostEstimate(flops=10**10, bytes_accessed=25 * 10**6, transcendentals=0),
        name="finish",
    )(where, count, x, c, *blocks, w_t, w_out)


def per_device(tokens, counts, w_qkv, w_out, cotangent):
    where = jnp.stack([lax.axis_index(a) for a in AXES]).astype(jnp.int32)
    x, c = tokens[0], cotangent[0]
    w_t = w_qkv.T
    ctx = lax.axis_index(CTX).astype(jnp.int32)
    heads = lambda places: ctx ^ jnp.array(places, jnp.int32)
    early = front(heads(EARLY), where, counts, x, c, w_t, w_out, False)
    *late, near, far = front(heads(LATE), where, counts, x, c, w_t, w_out, True)
    blocks = exchange(early, late)
    blocks, far = lax.optimization_barrier((blocks, far))
    far = other_core(far)
    made = attention(blocks)
    back = exchange([made[p] for p in EARLY], [made[p] for p in LATE])
    others = [other_core(b) for b in back]
    sums = weight_grads(where, near, far, *back, *others)
    back, sums = lax.optimization_barrier((back, sums))
    outs = finish(where, counts, x, c, back, w_t, w_out)
    share, (mixed, grad_tokens) = sum_over_chips(sums[:3], sums[3:], outs)

    share = jnp.concatenate([share[: 15 * 11], share[168 : 168 + 7 * 11]], axis=0)
    share = share.reshape(22, 11, 128).transpose(1, 0, 2).reshape(11, 22 * 128)
    wide = 3 * HEADS * HEAD_DIM
    return (mixed[None], grad_tokens[None], share[:, :wide], share[:, wide:].T)


def solution(mesh):
    split_mesh = Mesh(mesh.devices.reshape(4, 2, 2, 2, 4), AXES)
    dp, ctx = ("z", "yh", "core"), CTX
    return jax.shard_map(
        per_device,
        mesh=split_mesh,
        in_specs=(P(dp, ctx, None), P(dp, ctx), P(), P(), P(dp, ctx, None)),
        out_specs=(
            P(dp, ctx, None),
            P(dp, ctx, None),
            P(dp + ctx, None),
            P(None, dp + ctx),
        ),
        check_vma=False,
    )
```

```python
import functools

import jax
import jax.numpy as jnp
import numpy as np
from jax import lax
from jax.experimental import pallas as pl
from jax.experimental.pallas import tpu as pltpu
from jax.sharding import Mesh, PartitionSpec as P

HEADS = 8
HEAD_DIM = 88
SCALE = 1.0 / np.sqrt(np.float32(HEAD_DIM))
F32 = jnp.float32
BF16 = jnp.bfloat16
HIGH = lax.Precision.HIGH
AXES = ("z", "yh", "core", "yl", "x")
CTX = ("yl", "x")
FLIPS = ((3, 1), (1, 3))
PAIR = [(0, 1), (1, 0)]


def split(a):
    hi = a.astype(BF16)
    return hi, (a - hi.astype(F32)).astype(BF16)


def halves(a):
    hi = a.astype(BF16).astype(F32)
    return hi, a - hi


LEAST = 5
LANES = 128


def attention_kernel(*refs):
    ins, outs, scratch = refs[:8], refs[8:16], refs[16:]
    packed, rk, rv, kc, vc, s_ref, pp, ds, dk, dv = scratch
    d = HEAD_DIM
    n = ins[0].shape[2]
    live_row = 4 * d
    dot = functools.partial(jnp.dot, preferred_element_type=F32)
    group = lambda i: slice(i * LANES, (i + 1) * LANES)

    offset = [0]
    for block in ins:
        count = jnp.sum(block[0, live_row : live_row + 1]).astype(jnp.int32)
        offset.append(pl.multiple_of(offset[-1] + ((count + 7) & ~7), 8))
    top = lax.broadcasted_iota(jnp.int32, (8, n), 0) == 0
    zeros = lambda rows: jnp.zeros((rows, n), F32)
    for block, first in zip(ins, offset):
        r = block[0]
        one = jnp.where(top, 1.0, 0.0)
        dead = jnp.where(top, (r[live_row:] - 1.0) * 1e30, 0.0)
        pieces = [r[0:d], one, zeros(32), r[3 * d : 4 * d], zeros(40)]
        pieces += [r[d : 2 * d], dead, zeros(32), r[2 * d : 3 * d], zeros(40)]
        packed[pl.ds(first, n), :] = jnp.concatenate(pieces, axis=0).T
    lanes = lax.broadcasted_iota(jnp.int32, (n, 4 * LANES), 1)
    nothing = jnp.where(lanes == 2 * LANES + d, -1e30, 0.0)
    packed[pl.ds(offset[-1], n), :] = nothing
    used = jnp.maximum((offset[-1] + n - 1) // n, LEAST)
    for b in range(LEAST):

        @pl.when(offset[-1] <= b * n)
        def _(b=b):
            packed[b * n : (b + 1) * n, :] = nothing

    def at(b):
        return pl.ds(pl.multiple_of(b * n, n), n)

    def prepare(b, c):
        t = packed[at(b), 2 * LANES :].T
        for i, (wide, rows) in enumerate(((rk, kc), (rv, vc))):
            hi, lo = split(t[group(i)])
            wide[group(0), at(b)] = hi
            wide[group(1), at(b)] = hi
            wide[group(2), at(b)] = lo
            rows[at(b), group(0)], rows[at(b), group(1)] = split(packed[at(b), group(2 + i)])
        return c

    lax.fori_loop(0, used, prepare, 0)
    dk[...] = jnp.zeros_like(dk)
    dv[...] = jnp.zeros_like(dv)

    def stacked(a):
        hi, lo = halves(a.T)
        both = jnp.concatenate([hi[0:d], lo[0:d]], axis=0).astype(BF16)
        return jnp.concatenate([both, both], axis=1)

    def fold(a):
        a = a[0:n] + a[n:]
        return a[:, group(0)] + a[:, group(1)]

    def queries(blocks, j):
        keys = blocks * n
        cuts = (0, keys) if blocks != 7 else (0, keys - n, keys)
        spans = [slice(a, b) for a, b in zip(cuts, cuts[1:])]
        tiles = [slice(b * n, (b + 1) * n) for b in range(blocks)]
        q = packed[at(j), group(0)] * SCALE
        qh, ql = split(q)
        lq = jnp.concatenate([qh, ql, qh], axis=1)
        m = jnp.full((n, LANES), -1e30, F32)
        for t in tiles:
            s = dot(lq, rk[:, t])
            s_ref[:, t] = s
            m = jnp.maximum(m, jnp.maximum(s[:, group(0)], s[:, group(1)]))
        m = jnp.max(m, axis=1, keepdims=True)
        l = jnp.zeros((n, LANES), F32)
        for t in tiles:
            p = jnp.exp(s_ref[:, t] - m)
            s_ref[:, t] = p
            pp[0:n, t], pp[n:, t] = split(p)
            l = l + (p[:, group(0)] + p[:, group(1)])
        o = sum(dot(pp[:, s], vc[s, :]) for s in spans)
        rl = 1.0 / jnp.sum(l, axis=1, keepdims=True)
        o = fold(o) * rl
        g = packed[at(j), group(1)] * rl
        row_dot = jnp.sum(g * o, axis=1, keepdims=True)
        gh, gl = split(g)
        lg = jnp.concatenate([gh, gl, gh], axis=1)
        g2 = stacked(g)
        for s in spans:
            dv[:, s] += dot(g2, pp[:, s])
        for t in tiles:
            grad = s_ref[:, t] * (dot(lg, rv[:, t]) - row_dot)
            ds[0:n, t], ds[n:, t] = split(grad)
        q2 = stacked(q)
        for s in spans:
            dk[:, s] += dot(q2, ds[:, s])
        packed[at(j), group(0)] = o
        packed[at(j), group(1)] = fold(sum(dot(ds[:, s], kc[s, :]) for s in spans)) * SCALE

    def all_queries(blocks):
        def body(j, c):
            queries(blocks, j)
            return c

        lax.fori_loop(0, blocks, body, 0)

    for blocks in range(LEAST, 9):
        pl.when(used == blocks)(functools.partial(all_queries, blocks))

    def finish_keys(b, c):
        for i, ref in enumerate((dk, dv)):
            a = ref[:, at(b)]
            a = jnp.concatenate([a[0:d] + a[d:], zeros(40)], axis=0)
            packed[at(b), group(2 + i)] = a.T
        return c

    lax.fori_loop(0, used, finish_keys, 0)
    for block, first, out in zip(ins, offset, outs):
        rows = packed[pl.ds(first, n), :].T
        live = block[0, live_row : live_row + 1] > 0
        for k in range(4):
            out[0, k * d : (k + 1) * d] = jnp.where(live, rows[k * LANES : k * LANES + d], 0.0)


def attention(blocks):
    rows, n = blocks[0].shape[1:]
    d = HEAD_DIM
    total = 8 * n
    first = lambda a: pl.BlockSpec((1, rows, n), lambda i: (0, 0, 0))
    return pl.pallas_call(
        attention_kernel,
        grid=(1,),
        out_shape=[jax.ShapeDtypeStruct((1, 4 * d, n), F32)] * 8,
        in_specs=[first(b) for b in blocks],
        out_specs=[pl.BlockSpec((1, 4 * d, n), lambda i: (0, 0, 0))] * 8,
        scratch_shapes=[
            pltpu.VMEM((total + n, 4 * LANES), F32),
            pltpu.VMEM((3 * LANES, total), BF16),
            pltpu.VMEM((3 * LANES, total), BF16),
            pltpu.VMEM((total, 2 * LANES), BF16),
            pltpu.VMEM((total, 2 * LANES), BF16),
            pltpu.VMEM((n, total), F32),
            pltpu.VMEM((2 * n, total), BF16),
            pltpu.VMEM((2 * n, total), BF16),
            pltpu.VMEM((2 * d, total), F32),
            pltpu.VMEM((2 * d, total), F32),
        ],
        compiler_params=pltpu.CompilerParams(vmem_limit_bytes=52 * 2**20),
        name="attention",
    )(*blocks)


PART_TILES = (8, 7, 7)
PART_ROWS = (88, 80, 80)
PART_RINGS = ((2, 1, 0), (1, 0, 2), (0, 2, 1))


def weights_kernel(where, near, far, *refs):
    own, other, refs = refs[:8], refs[8:16], refs[16:]
    results, made, (n3, m3, g3, a3, w, grads, done) = refs[:6], refs[6:12], refs[12:]
    sends, keeps = made[:3], made[3:]
    d = HEAD_DIM
    half = near.shape[3]
    rows = near.shape[1] * d
    wide = HEADS * d
    z, yh, core, yl, x = [where[i] for i in range(5)]

    def keep(at, to, lo, pieces):
        for i, p in enumerate(pieces):
            h, l = split(p)
            for k in range(3):
                to[at, (2 * k + i) * half : (2 * k + i + 1) * half] = (h, l)[k == lo]

    keep(slice(0, rows), n3, 2, [r[0].reshape(rows, half) for r in (near, far)])
    keep(slice(0, rows), m3, 2, [r[1].reshape(rows, half) for r in (near, far)])
    for i, blocks in enumerate((own, other)):
        for p, block in enumerate(blocks):
            grads[(yl * 4 + x) ^ p, :, i * half : (i + 1) * half] = block[0]

    def prepare(kind):
        for pair in range(HEADS // 2):
            pieces = [
                jnp.concatenate(
                    [
                        grads[2 * pair + k, kind * d : (kind + 1) * d, i * half : (i + 1) * half]
                        for k in range(2)
                    ],
                    axis=0,
                )
                for i in range(2)
            ]
            first = ((kind - 1) * wide if kind else 0) + 2 * pair * d
            keep(slice(first, first + 2 * d), g3 if kind else a3, 1, pieces)

    prepare(1)
    prepare(2)
    w[:, 0:768] = dot_rows(n3[...], g3[0:768, :])
    prepare(3)
    w[:, 768:1536] = dot_rows(n3[...], g3[768:1536, :])
    prepare(0)
    w[:, 1536 : 3 * wide] = dot_rows(n3[...], g3[1536:, :])
    w[:, 3 * wide :] = dot_rows(m3[...], a3[...])

    for refs in (sends, keeps):
        for ref in refs[1:]:
            ref[:, :, :, 72:80, :] = jnp.zeros((2, 2, 8, 8, 128), F32)

    def bits(own, to):
        p = own ^ to
        first = jnp.where(core == 0, p >> 1, (p ^ (p >> 1)) & 1)
        return first, jnp.where(core == 0, to & 1, to >> 1)

    def scatter(part, tile, zy, carry):
        at = pl.ds(pl.multiple_of(zy * d, 8), d)
        r0, r1, r2 = PART_RINGS[part]
        z_bits = bits(z, zy >> 1)
        for c in range(8):
            y_bits = bits((yh << 1) | yl, ((zy & 1) << 1) | (c >> 2))
            x_bits = bits(x, c & 3)
            a = (z_bits[0], y_bits[0], x_bits[0])
            j = (z_bits[1] << 2) | (y_bits[1] << 1) | x_bits[1]

            def store(ref, a=a, j=j, c=c):
                for t in range(PART_TILES[part]):
                    block = w[at, (tile + t) * 128 : (tile + t + 1) * 128]
                    ref[a[r1], a[r2], j, t * 11 : (t + 1) * 11, :] = block[c * 11 : (c + 1) * 11]

            pl.when(a[r0] == 1)(functools.partial(store, sends[part]))
            pl.when(a[r0] == 0)(functools.partial(store, keeps[part]))
        return carry

    copies = [pltpu.make_async_copy(m, r, done.at[i]) for i, (m, r) in enumerate(zip(made, results))]
    for part in range(3):
        lax.fori_loop(0, 8, functools.partial(scatter, part, sum(PART_TILES[:part])), 0)
        copies[part].start()
        copies[3 + part].start()
    for copy in copies:
        copy.wait()


def weight_grads(where, *arrays):
    _, blocks, _, half = arrays[0].shape
    rows = blocks * HEAD_DIM
    wide = HEADS * HEAD_DIM
    vmem = pl.BlockSpec(memory_space=pltpu.VMEM)
    return pl.pallas_call(
        weights_kernel,
        in_specs=[pl.BlockSpec(memory_space=pltpu.SMEM)] + [vmem] * len(arrays),
        out_specs=[pl.BlockSpec(memory_space=pl.ANY)] * 6,
        out_shape=[jax.ShapeDtypeStruct((2, 2, 8, r, 128), F32) for r in PART_ROWS] * 2,
        scratch_shapes=[pltpu.VMEM((2, 2, 8, r, 128), F32) for r in PART_ROWS] * 2
        + [
            pltpu.VMEM((rows, 6 * half), BF16),
            pltpu.VMEM((rows, 6 * half), BF16),
            pltpu.VMEM((3 * wide, 6 * half), BF16),
            pltpu.VMEM((wide, 6 * half), BF16),
            pltpu.VMEM((rows, 4 * wide), F32),
            pltpu.VMEM((HEADS, 4 * HEAD_DIM, 2 * half), F32),
            pltpu.SemaphoreType.DMA((6,)),
        ],
        compiler_params=pltpu.CompilerParams(vmem_limit_bytes=56 * 2**20),
        name="weight_grads",
    )(where, *arrays)


def index_of(z, y, core, x):
    return (((z * 2 + (y >> 1)) * 2 + core) * 2 + (y & 1)) * 4 + x


def swap_over(piece, flips, which):
    pairs = []
    for z in range(4):
        for y in range(4):
            for core in range(2):
                f = FLIPS[core][which]
                for x in range(4):
                    to = index_of(z ^ (f * flips[0]), y ^ (f * flips[1]), core, x ^ (f * flips[2]))
                    pairs.append((index_of(z, y, core, x), to))
    return lax.ppermute(piece, AXES, pairs)


def sum_over_chips(sends, keeps, beside):
    flips = lambda r: [int(r == k) for k in range(3)]
    sent = lax.optimization_barrier(list(sends))
    got = [swap_over(s, flips(r[0]), 0) for s, r in zip(sent, PART_RINGS)]
    got, beside = lax.optimization_barrier((got, beside))
    kept = list(keeps)
    for step in (1, 2):
        sent = lax.optimization_barrier([k[1] + g[1] for k, g in zip(kept, got)])
        kept = [k[0] + g[0] for k, g in zip(kept, got)]
        got = [swap_over(s, flips(r[step]), 0) for s, r in zip(sent, PART_RINGS)]
        got = lax.optimization_barrier(got)
    rest = jnp.concatenate([k + g for k, g in zip(kept, got)], axis=1)
    got = lax.all_to_all(rest, AXES, 0, 0, axis_index_groups=last_groups(), tiled=True)
    return jnp.sum(got, axis=0), beside


def last_groups():
    groups = {}
    for z in range(4):
        for y in range(4):
            for core in range(2):
                for x in range(4):
                    kept = lambda i: (i ^ (i >> 1)) & 1 if core else i >> 1
                    label = lambda i: i >> 1 if core else i & 1
                    key = (core, kept(z), kept(y), kept(x))
                    groups.setdefault(key, []).append(((label(z), label(y), label(x)), index_of(z, y, core, x)))
    return [[i for _, i in sorted(g)] for g in groups.values()]


def exchange(early, late):
    send = lambda a, p: lax.ppermute(a, CTX, [(i, i ^ p) for i in range(8)])
    b2, b6, b5, b7 = early
    g2, g6, r5, r7 = send(b2, 1), send(b6, 3), send(b5, 5), send(b7, 7)
    g2, g6, late = lax.optimization_barrier((g2, g6, late))
    b0, b1, b3, b4 = late
    f2, f6 = send(g2, 3), send(g6, 5)
    return [b0, send(b1, 1), f2, send(b3, 3), send(b4, 4), r5, f6, r7]


def other_core(a):
    return lax.ppermute(a, "core", PAIR)


def layer_norm(x):
    centred = x - jnp.sum(x, axis=1, keepdims=True) / x.shape[1]
    var = jnp.sum(centred * centred, axis=1, keepdims=True) / x.shape[1]
    inv_std = lax.rsqrt(var + 1e-06)
    return centred * inv_std, inv_std


def masked_rows(ref, count):
    rows = lax.broadcasted_iota(jnp.int32, ref.shape, 0)
    return jnp.where(rows < count[0, 0], ref[...], 0.0)


def dot_rows(a, b):
    return lax.dot_general(a, b, (((1,), (1,)), ((), ())), preferred_element_type=F32)


EARLY = (2, 6, 5, 7)
LATE = (0, 1, 3, 4)


def whole(a):
    return pl.BlockSpec(a.shape, lambda *i: (0,) * len(a.shape))


def front_kernel(features, where, count, x_ref, c_ref, q_ref, k_ref, v_ref, o_ref, *refs):
    messages, refs = refs[:4], refs[4:]
    nh, nl, mh, ml = refs[-4:]
    d = HEAD_DIM
    slots = x_ref.shape[0]
    step = pl.program_id(0)

    @pl.when(step == 0)
    def _():
        normed, _ = layer_norm(x_ref[...])
        masked = masked_rows(c_ref, count)
        nh[...], nl[...] = split(normed)
        mh[...], ml[...] = split(masked)
        if features:
            near, far, turned = refs[:3]
            core = where[2]
            for k, a in enumerate((normed, masked)):
                turned[...] = a.T
                for i in range(8):
                    for ref, c in ((near, core), (far, 1 - core)):
                        ref[k, i] = turned[pl.ds(pl.multiple_of((2 * i + c) * d, 8), d), :]

    def project(w, hi, lo):
        rows = w.shape[0]
        wh, wl = halves(w)
        both = dot_rows(jnp.concatenate([wh, wl], axis=0).astype(BF16), hi[...])
        return both[0:rows] + (both[rows:] + dot_rows(wh.astype(BF16), lo[...]))

    qkv = project(jnp.concatenate([q_ref[...], k_ref[...], v_ref[...]], axis=0), nh, nl)
    grads = project(o_ref[...], mh, ml)
    lanes = lax.broadcasted_iota(jnp.int32, (8, slots), 1)
    for i, message in enumerate(messages):

        @pl.when(step == i)
        def _(message=message):
            message[0, 0 : 3 * d, :] = qkv
            message[0, 3 * d : 4 * d, :] = grads
            message[0, 4 * d :, :] = (lanes < count[0, 0]).astype(F32)


def front(places, features, where, count, x, c, w_t, w_out):
    slots, width = x.shape
    d = HEAD_DIM

    def part(kind):
        def index(i, where, count):
            p = places[0]
            for k in range(1, 4):
                p = jnp.where(i == k, places[k], p)
            return kind * HEADS + ((where[3] * 4 + where[4]) ^ p), 0

        return pl.BlockSpec((d, width), index)

    outs = [jax.ShapeDtypeStruct((1, 4 * d + 8, slots), F32)] * 4
    scratch = [pltpu.VMEM((slots, width), BF16)] * 4
    if features:
        outs += [jax.ShapeDtypeStruct((2, 8, d, slots), F32)] * 2
        scratch = [pltpu.VMEM((width, slots), F32)] + scratch
    return pl.pallas_call(
        functools.partial(front_kernel, features),
        grid_spec=pltpu.PrefetchScalarGridSpec(
            num_scalar_prefetch=2,
            grid=(4,),
            in_specs=[whole(x), whole(c), part(0), part(1), part(2), part(0)],
            out_specs=[whole(a) for a in outs],
            scratch_shapes=scratch,
        ),
        out_shape=outs,
        compiler_params=pltpu.CompilerParams(vmem_limit_bytes=58 * 2**20),
        cost_estimate=pl.CostEstimate(flops=6 * 10**9, bytes_accessed=14 * 10**6, transcendentals=0),
        name="front",
    )(where, count, x, c, w_t, w_t, w_t, w_out)


def finish_kernel(where, count, x_ref, c_ref, *refs):
    blocks, (w_ref, o_ref, mixed, grad, g2, acc, turned) = refs[:8], refs[8:]
    d = HEAD_DIM
    wide = HEADS * d
    slots, width = x_ref.shape
    step = pl.program_id(0)

    @pl.when(step == 0)
    def _():
        for p, block in enumerate(blocks):
            head = (where[3] * 4 + where[4]) ^ p
            for kind in range(4):
                at = pl.ds(pl.multiple_of(head * d + kind * wide, 8), d)
                turned[at, :] = block[0, kind * d : (kind + 1) * d]
        g2[0:slots, :], g2[slots:, :] = split(turned[wide:, :].T)
        ah, al = split(turned[0:wide, :].T)
        oh, ol = split(o_ref[...])
        r = jnp.dot(jnp.concatenate([ah, al], axis=0), oh, preferred_element_type=F32)
        r2 = jnp.dot(ah, ol, preferred_element_type=F32)
        rows = lax.broadcasted_iota(jnp.int32, x_ref.shape, 0)
        projected = r[0:slots] + (r[slots:] + r2)
        mixed[...] = jnp.where(rows < count[0, 0], x_ref[...] + projected, 0.0)

    wh, wl = split(w_ref[...])
    r = jnp.dot(g2[...], wh, preferred_element_type=F32)
    r2 = jnp.dot(g2[0:slots, :], wl, preferred_element_type=F32)
    acc[step] = r[0:slots] + (r[slots:] + r2)

    @pl.when(step == pl.num_programs(0) - 1)
    def _():
        g = jnp.concatenate([acc[i] for i in range(acc.shape[0])], axis=1)[:, 0:width]
        normed, inv_std = layer_norm(x_ref[...])
        mean = jnp.sum(g, axis=1, keepdims=True) / width
        along = jnp.sum(g * normed, axis=1, keepdims=True) / width
        grad[...] = masked_rows(c_ref, count) + inv_std * (g - mean - normed * along)


def finish(where, count, x, c, blocks, w_t, w_out):
    slots, width = x.shape
    smem = pl.BlockSpec(memory_space=pltpu.SMEM)
    step = 512
    steps = -(-width // step)
    columns = w_t.shape[0]
    first = lambda a: pl.BlockSpec((1,) + a.shape[1:], lambda i: (0, 0, 0))
    return pl.pallas_call(
        finish_kernel,
        grid=(steps,),
        in_specs=[smem, smem, whole(x), whole(c)]
        + [first(b) for b in blocks]
        + [pl.BlockSpec((columns, step), lambda i: (0, i)), whole(w_out)],
        out_specs=[whole(x), whole(x)],
        out_shape=[jax.ShapeDtypeStruct(x.shape, F32)] * 2,
        scratch_shapes=[
            pltpu.VMEM((2 * slots, columns), BF16),
            pltpu.VMEM((steps, slots, step), F32),
            pltpu.VMEM((4 * HEADS * HEAD_DIM, slots), F32),
        ],
        compiler_params=pltpu.CompilerParams(vmem_limit_bytes=56 * 2**20),
        cost_estimate=pl.CostEstimate(flops=10**10, bytes_accessed=25 * 10**6, transcendentals=0),
        name="finish",
    )(where, count, x, c, *blocks, w_t, w_out)


def per_device(tokens, counts, w_qkv, w_out, cotangent):
    where = jnp.stack([lax.axis_index(a) for a in AXES]).astype(jnp.int32)
    x, c = tokens[0], cotangent[0]
    w_t = w_qkv.T
    early = front(EARLY, False, where, counts, x, c, w_t, w_out)
    *late, near, far = front(LATE, True, where, counts, x, c, w_t, w_out)
    blocks = exchange(early, late)
    blocks, far = lax.optimization_barrier((blocks, far))
    far = other_core(far)
    made = attention(blocks)
    back = exchange([made[p] for p in EARLY], [made[p] for p in LATE])
    others = [other_core(b) for b in back]
    sums = weight_grads(where, near, far, *back, *others)
    back, sums = lax.optimization_barrier((back, sums))
    outs = finish(where, counts, x, c, back, w_t, w_out)
    share, (mixed, grad_tokens) = sum_over_chips(sums[:3], sums[3:], outs)

    share = jnp.concatenate([share[: 15 * 11], share[168 : 168 + 7 * 11]], axis=0)
    share = share.reshape(22, 11, 128).transpose(1, 0, 2).reshape(11, 22 * 128)
    wide = 3 * HEADS * HEAD_DIM
    return (mixed[None], grad_tokens[None], share[:, :wide], share[:, wide:].T)


def solution(mesh):
    split_mesh = Mesh(mesh.devices.reshape(4, 2, 2, 2, 4), AXES)
    dp, ctx = ("z", "yh", "core"), CTX
    return jax.shard_map(
        per_device,
        mesh=split_mesh,
        in_specs=(P(dp, ctx, None), P(dp, ctx), P(), P(), P(dp, ctx, None)),
        out_specs=(
            P(dp, ctx, None),
            P(dp, ctx, None),
            P(dp + ctx, None),
            P(None, dp + ctx),
        ),
        check_vma=False,
    )
```

```python
import functools

import jax
import jax.numpy as jnp
import numpy as np
from jax import lax
from jax.experimental import pallas as pl
from jax.experimental.pallas import tpu as pltpu
from jax.sharding import Mesh, PartitionSpec as P

HEADS = 8
HEAD_DIM = 88
SCALE = 1.0 / np.sqrt(np.float32(HEAD_DIM))
F32 = jnp.float32
BF16 = jnp.bfloat16
AXES = ("z", "yh", "core", "yl", "x")
CTX = ("yl", "x")
FLIPS = ((3, 1), (1, 3))
PAIR = [(0, 1), (1, 0)]


def split(a):
    hi = a.astype(BF16)
    return hi, (a - hi.astype(F32)).astype(BF16)


def halves(a):
    hi = a.astype(BF16).astype(F32)
    return hi, a - hi


LEAST = 5
LANES = 128


def attention_kernel(*refs):
    ins, outs, scratch = refs[:8], refs[8:16], refs[16:]
    packed, rk, rv, kc, vc, s_ref, pp, ds, dk, dv = scratch
    d = HEAD_DIM
    n = ins[0].shape[2]
    live_row = 4 * d
    dot = functools.partial(jnp.dot, preferred_element_type=F32)
    group = lambda i: slice(i * LANES, (i + 1) * LANES)

    offset = [0]
    for block in ins:
        count = jnp.sum(block[0, live_row : live_row + 1]).astype(jnp.int32)
        offset.append(pl.multiple_of(offset[-1] + ((count + 7) & ~7), 8))
    top = lax.broadcasted_iota(jnp.int32, (8, n), 0) == 0
    zeros = lambda rows: jnp.zeros((rows, n), F32)
    for block, first in zip(ins, offset):
        r = block[0]
        one = jnp.where(top, 1.0, 0.0)
        dead = jnp.where(top, (r[live_row:] - 1.0) * 1e30, 0.0)
        pieces = [r[0:d], one, zeros(32), r[3 * d : 4 * d], zeros(40)]
        pieces += [r[d : 2 * d], dead, zeros(32), r[2 * d : 3 * d], zeros(40)]
        packed[pl.ds(first, n), :] = jnp.concatenate(pieces, axis=0).T
    lanes = lax.broadcasted_iota(jnp.int32, (n, 4 * LANES), 1)
    nothing = jnp.where(lanes == 2 * LANES + d, -1e30, 0.0)
    packed[pl.ds(offset[-1], n), :] = nothing
    used = jnp.maximum((offset[-1] + n - 1) // n, LEAST)
    for b in range(LEAST):

        @pl.when(offset[-1] <= b * n)
        def _(b=b):
            packed[b * n : (b + 1) * n, :] = nothing

    def at(b):
        return pl.ds(pl.multiple_of(b * n, n), n)

    def prepare(b, c):
        t = packed[at(b), 2 * LANES :].T
        for i, (wide, rows) in enumerate(((rk, kc), (rv, vc))):
            hi, lo = split(t[group(i)])
            wide[group(0), at(b)] = hi
            wide[group(1), at(b)] = hi
            wide[group(2), at(b)] = lo
            rows[at(b), group(0)], rows[at(b), group(1)] = split(packed[at(b), group(2 + i)])
        return c

    lax.fori_loop(0, used, prepare, 0)
    dk[...] = jnp.zeros_like(dk)
    dv[...] = jnp.zeros_like(dv)

    def stacked(a):
        hi, lo = halves(a.T)
        both = jnp.concatenate([hi[0:d], lo[0:d]], axis=0).astype(BF16)
        return jnp.concatenate([both, both], axis=1)

    def fold(a):
        a = a[0:n] + a[n:]
        return a[:, group(0)] + a[:, group(1)]

    def queries(blocks, j):
        keys = blocks * n
        cuts = (0, keys) if blocks != 7 else (0, keys - n, keys)
        spans = [slice(a, b) for a, b in zip(cuts, cuts[1:])]
        tiles = [slice(b * n, (b + 1) * n) for b in range(blocks)]
        q = packed[at(j), group(0)] * SCALE
        qh, ql = split(q)
        lq = jnp.concatenate([qh, ql, qh], axis=1)
        m = jnp.full((n, LANES), -1e30, F32)
        for t in tiles:
            s = dot(lq, rk[:, t])
            s_ref[:, t] = s
            m = jnp.maximum(m, jnp.maximum(s[:, group(0)], s[:, group(1)]))
        m = jnp.max(m, axis=1, keepdims=True)
        l = jnp.zeros((n, LANES), F32)
        for t in tiles:
            p = jnp.exp(s_ref[:, t] - m)
            s_ref[:, t] = p
            pp[0:n, t], pp[n:, t] = split(p)
            l = l + (p[:, group(0)] + p[:, group(1)])
        o = sum(dot(pp[:, s], vc[s, :]) for s in spans)
        rl = 1.0 / jnp.sum(l, axis=1, keepdims=True)
        o = fold(o) * rl
        g = packed[at(j), group(1)] * rl
        row_dot = jnp.sum(g * o, axis=1, keepdims=True)
        gh, gl = split(g)
        lg = jnp.concatenate([gh, gl, gh], axis=1)
        g2 = stacked(g)
        for s in spans:
            dv[:, s] += dot(g2, pp[:, s])
        for t in tiles:
            grad = s_ref[:, t] * (dot(lg, rv[:, t]) - row_dot)
            ds[0:n, t], ds[n:, t] = split(grad)
        q2 = stacked(q)
        for s in spans:
            dk[:, s] += dot(q2, ds[:, s])
        packed[at(j), group(0)] = o
        packed[at(j), group(1)] = fold(sum(dot(ds[:, s], kc[s, :]) for s in spans)) * SCALE

    def all_queries(blocks):
        def body(j, c):
            queries(blocks, j)
            return c

        lax.fori_loop(0, blocks, body, 0)

    for blocks in range(LEAST, 9):
        pl.when(used == blocks)(functools.partial(all_queries, blocks))

    def finish_keys(b, c):
        for i, ref in enumerate((dk, dv)):
            a = ref[:, at(b)]
            a = jnp.concatenate([a[0:d] + a[d:], zeros(40)], axis=0)
            packed[at(b), group(2 + i)] = a.T
        return c

    lax.fori_loop(0, used, finish_keys, 0)
    for block, first, out in zip(ins, offset, outs):
        rows = packed[pl.ds(first, n), :].T
        live = block[0, live_row : live_row + 1] > 0
        for k in range(4):
            out[0, k * d : (k + 1) * d] = jnp.where(live, rows[k * LANES : k * LANES + d], 0.0)


def attention(blocks):
    rows, n = blocks[0].shape[1:]
    d = HEAD_DIM
    total = 8 * n
    first = lambda a: pl.BlockSpec((1, rows, n), lambda i: (0, 0, 0))
    return pl.pallas_call(
        attention_kernel,
        grid=(1,),
        out_shape=[jax.ShapeDtypeStruct((1, 4 * d, n), F32)] * 8,
        in_specs=[first(b) for b in blocks],
        out_specs=[pl.BlockSpec((1, 4 * d, n), lambda i: (0, 0, 0))] * 8,
        scratch_shapes=[
            pltpu.VMEM((total + n, 4 * LANES), F32),
            pltpu.VMEM((3 * LANES, total), BF16),
            pltpu.VMEM((3 * LANES, total), BF16),
            pltpu.VMEM((total, 2 * LANES), BF16),
            pltpu.VMEM((total, 2 * LANES), BF16),
            pltpu.VMEM((n, total), F32),
            pltpu.VMEM((2 * n, total), BF16),
            pltpu.VMEM((2 * n, total), BF16),
            pltpu.VMEM((2 * d, total), F32),
            pltpu.VMEM((2 * d, total), F32),
        ],
        compiler_params=pltpu.CompilerParams(vmem_limit_bytes=52 * 2**20),
        name="attention",
    )(*blocks)


PART_TILES = (8, 7, 7)
PART_ROWS = (88, 80, 80)
PART_RINGS = ((2, 1, 0), (1, 0, 2), (0, 2, 1))


def weights_kernel(where, near, far, *refs):
    own, other, refs = refs[:8], refs[8:16], refs[16:]
    results, made, (n3, m3, g3, a3, w, grads, done) = refs[:6], refs[6:12], refs[12:]
    sends, keeps = made[:3], made[3:]
    d = HEAD_DIM
    half = near.shape[3]
    rows = near.shape[1] * d
    wide = HEADS * d
    z, yh, core, yl, x = [where[i] for i in range(5)]

    def keep(at, to, lo, pieces):
        for i, p in enumerate(pieces):
            h, l = split(p)
            for k in range(3):
                to[at, (2 * k + i) * half : (2 * k + i + 1) * half] = (h, l)[k == lo]

    keep(slice(0, rows), n3, 2, [r[0].reshape(rows, half) for r in (near, far)])
    keep(slice(0, rows), m3, 2, [r[1].reshape(rows, half) for r in (near, far)])
    for i, blocks in enumerate((own, other)):
        for p, block in enumerate(blocks):
            grads[(yl * 4 + x) ^ p, :, i * half : (i + 1) * half] = block[0]

    def prepare(kind):
        for pair in range(HEADS // 2):
            pieces = [
                jnp.concatenate(
                    [
                        grads[2 * pair + k, kind * d : (kind + 1) * d, i * half : (i + 1) * half]
                        for k in range(2)
                    ],
                    axis=0,
                )
                for i in range(2)
            ]
            first = ((kind - 1) * wide if kind else 0) + 2 * pair * d
            keep(slice(first, first + 2 * d), g3 if kind else a3, 1, pieces)

    prepare(1)
    prepare(2)
    w[:, 0:768] = dot_rows(n3[...], g3[0:768, :])
    prepare(3)
    w[:, 768:1536] = dot_rows(n3[...], g3[768:1536, :])
    prepare(0)
    w[:, 1536 : 3 * wide] = dot_rows(n3[...], g3[1536:, :])
    w[:, 3 * wide :] = dot_rows(m3[...], a3[...])

    for refs in (sends, keeps):
        for ref in refs[1:]:
            ref[:, :, :, 72:80, :] = jnp.zeros((2, 2, 8, 8, 128), F32)

    def bits(own, to):
        p = own ^ to
        first = jnp.where(core == 0, p >> 1, (p ^ (p >> 1)) & 1)
        return first, jnp.where(core == 0, to & 1, to >> 1)

    def scatter(part, tile, zy, carry):
        at = pl.ds(pl.multiple_of(zy * d, 8), d)
        r0, r1, r2 = PART_RINGS[part]
        z_bits = bits(z, zy >> 1)
        for c in range(8):
            y_bits = bits((yh << 1) | yl, ((zy & 1) << 1) | (c >> 2))
            x_bits = bits(x, c & 3)
            a = (z_bits[0], y_bits[0], x_bits[0])
            j = (z_bits[1] << 2) | (y_bits[1] << 1) | x_bits[1]

            def store(ref, a=a, j=j, c=c):
                for t in range(PART_TILES[part]):
                    block = w[at, (tile + t) * 128 : (tile + t + 1) * 128]
                    ref[a[r1], a[r2], j, t * 11 : (t + 1) * 11, :] = block[c * 11 : (c + 1) * 11]

            pl.when(a[r0] == 1)(functools.partial(store, sends[part]))
            pl.when(a[r0] == 0)(functools.partial(store, keeps[part]))
        return carry

    copies = [pltpu.make_async_copy(m, r, done.at[i]) for i, (m, r) in enumerate(zip(made, results))]
    for part in range(3):
        lax.fori_loop(0, 8, functools.partial(scatter, part, sum(PART_TILES[:part])), 0)
        copies[part].start()
        copies[3 + part].start()
    for copy in copies:
        copy.wait()


def weight_grads(where, *arrays):
    _, blocks, _, half = arrays[0].shape
    rows = blocks * HEAD_DIM
    wide = HEADS * HEAD_DIM
    vmem = pl.BlockSpec(memory_space=pltpu.VMEM)
    return pl.pallas_call(
        weights_kernel,
        in_specs=[pl.BlockSpec(memory_space=pltpu.SMEM)] + [vmem] * len(arrays),
        out_specs=[pl.BlockSpec(memory_space=pl.ANY)] * 6,
        out_shape=[jax.ShapeDtypeStruct((2, 2, 8, r, 128), F32) for r in PART_ROWS] * 2,
        scratch_shapes=[pltpu.VMEM((2, 2, 8, r, 128), F32) for r in PART_ROWS] * 2
        + [
            pltpu.VMEM((rows, 6 * half), BF16),
            pltpu.VMEM((rows, 6 * half), BF16),
            pltpu.VMEM((3 * wide, 6 * half), BF16),
            pltpu.VMEM((wide, 6 * half), BF16),
            pltpu.VMEM((rows, 4 * wide), F32),
            pltpu.VMEM((HEADS, 4 * HEAD_DIM, 2 * half), F32),
            pltpu.SemaphoreType.DMA((6,)),
        ],
        compiler_params=pltpu.CompilerParams(vmem_limit_bytes=56 * 2**20),
        name="weight_grads",
    )(where, *arrays)


def index_of(z, y, core, x):
    return (((z * 2 + (y >> 1)) * 2 + core) * 2 + (y & 1)) * 4 + x


def swap_over(piece, flips, which):
    pairs = []
    for z in range(4):
        for y in range(4):
            for core in range(2):
                f = FLIPS[core][which]
                for x in range(4):
                    to = index_of(z ^ (f * flips[0]), y ^ (f * flips[1]), core, x ^ (f * flips[2]))
                    pairs.append((index_of(z, y, core, x), to))
    return lax.ppermute(piece, AXES, pairs)


def sum_over_chips(sends, keeps, beside):
    flips = lambda r: [int(r == k) for k in range(3)]
    sent = lax.optimization_barrier(list(sends))
    got = [swap_over(s, flips(r[0]), 0) for s, r in zip(sent, PART_RINGS)]
    got, beside = lax.optimization_barrier((got, beside))
    kept = list(keeps)
    for step in (1, 2):
        sent = lax.optimization_barrier([k[1] + g[1] for k, g in zip(kept, got)])
        kept = [k[0] + g[0] for k, g in zip(kept, got)]
        got = [swap_over(s, flips(r[step]), 0) for s, r in zip(sent, PART_RINGS)]
        got = lax.optimization_barrier(got)
    rest = jnp.concatenate([k + g for k, g in zip(kept, got)], axis=1)
    got = lax.all_to_all(rest, AXES, 0, 0, axis_index_groups=last_groups(), tiled=True)
    return jnp.sum(got, axis=0), beside


def last_groups():
    groups = {}
    for z in range(4):
        for y in range(4):
            for core in range(2):
                for x in range(4):
                    kept = lambda i: (i ^ (i >> 1)) & 1 if core else i >> 1
                    label = lambda i: i >> 1 if core else i & 1
                    key = (core, kept(z), kept(y), kept(x))
                    groups.setdefault(key, []).append(((label(z), label(y), label(x)), index_of(z, y, core, x)))
    return [[i for _, i in sorted(g)] for g in groups.values()]


def exchange(early, late):
    send = lambda a, p: lax.ppermute(a, CTX, [(i, i ^ p) for i in range(8)])
    b2, b6, b5, b7 = early
    g2, g6, r5, r7 = send(b2, 1), send(b6, 3), send(b5, 5), send(b7, 7)
    g2, g6, late = lax.optimization_barrier((g2, g6, late))
    b0, b1, b3, b4 = late
    f2, f6 = send(g2, 3), send(g6, 5)
    return [b0, send(b1, 1), f2, send(b3, 3), send(b4, 4), r5, f6, r7]


def other_core(a):
    return lax.ppermute(a, "core", PAIR)


def layer_norm(x):
    centred = x - jnp.sum(x, axis=1, keepdims=True) / x.shape[1]
    var = jnp.sum(centred * centred, axis=1, keepdims=True) / x.shape[1]
    inv_std = lax.rsqrt(var + 1e-06)
    return centred * inv_std, inv_std


def masked_rows(ref, count):
    rows = lax.broadcasted_iota(jnp.int32, ref.shape, 0)
    return jnp.where(rows < count[0, 0], ref[...], 0.0)


def dot_rows(a, b):
    return lax.dot_general(a, b, (((1,), (1,)), ((), ())), preferred_element_type=F32)


EARLY = (2, 6, 5, 7)
LATE = (0, 1, 3, 4)


def whole(a):
    return pl.BlockSpec(a.shape, lambda *i: (0,) * len(a.shape))


def front_kernel(features, where, count, x_ref, c_ref, q_ref, k_ref, v_ref, o_ref, *refs):
    messages, refs = refs[:4], refs[4:]
    nh, nl, mh, ml = refs[-4:]
    d = HEAD_DIM
    slots = x_ref.shape[0]
    step = pl.program_id(0)

    @pl.when(step == 0)
    def _():
        normed, _ = layer_norm(x_ref[...])
        masked = masked_rows(c_ref, count)
        nh[...], nl[...] = split(normed)
        mh[...], ml[...] = split(masked)
        if features:
            near, far, turned = refs[:3]
            core = where[2]
            for k, a in enumerate((normed, masked)):
                turned[...] = a.T
                for i in range(8):
                    for ref, c in ((near, core), (far, 1 - core)):
                        ref[k, i] = turned[pl.ds(pl.multiple_of((2 * i + c) * d, 8), d), :]

    def project(w, hi, lo):
        rows = w.shape[0]
        wh, wl = halves(w)
        both = dot_rows(jnp.concatenate([wh, wl], axis=0).astype(BF16), hi[...])
        return both[0:rows] + (both[rows:] + dot_rows(wh.astype(BF16), lo[...]))

    qkv = project(jnp.concatenate([q_ref[...], k_ref[...], v_ref[...]], axis=0), nh, nl)
    grads = project(o_ref[...], mh, ml)
    lanes = lax.broadcasted_iota(jnp.int32, (8, slots), 1)
    for i, message in enumerate(messages):

        @pl.when(step == i)
        def _(message=message):
            message[0, 0 : 3 * d, :] = qkv
            message[0, 3 * d : 4 * d, :] = grads
            message[0, 4 * d :, :] = (lanes < count[0, 0]).astype(F32)


def front(places, features, where, count, x, c, w_t, w_out):
    slots, width = x.shape
    d = HEAD_DIM

    def part(kind):
        def index(i, where, count):
            p = places[0]
            for k in range(1, 4):
                p = jnp.where(i == k, places[k], p)
            return kind * HEADS + ((where[3] * 4 + where[4]) ^ p), 0

        return pl.BlockSpec((d, width), index)

    outs = [jax.ShapeDtypeStruct((1, 4 * d + 8, slots), F32)] * 4
    scratch = [pltpu.VMEM((slots, width), BF16)] * 4
    if features:
        outs += [jax.ShapeDtypeStruct((2, 8, d, slots), F32)] * 2
        scratch = [pltpu.VMEM((width, slots), F32)] + scratch
    return pl.pallas_call(
        functools.partial(front_kernel, features),
        grid_spec=pltpu.PrefetchScalarGridSpec(
            num_scalar_prefetch=2,
            grid=(4,),
            in_specs=[whole(x), whole(c), part(0), part(1), part(2), part(0)],
            out_specs=[whole(a) for a in outs],
            scratch_shapes=scratch,
        ),
        out_shape=outs,
        compiler_params=pltpu.CompilerParams(vmem_limit_bytes=58 * 2**20),
        cost_estimate=pl.CostEstimate(flops=6 * 10**9, bytes_accessed=14 * 10**6, transcendentals=0),
        name="front",
    )(where, count, x, c, w_t, w_t, w_t, w_out)


def finish_kernel(where, count, x_ref, c_ref, *refs):
    blocks, (w_ref, o_ref, mixed, grad, g2, acc, turned) = refs[:8], refs[8:]
    d = HEAD_DIM
    wide = HEADS * d
    slots, width = x_ref.shape
    step = pl.program_id(0)

    @pl.when(step == 0)
    def _():
        for p, block in enumerate(blocks):
            head = (where[3] * 4 + where[4]) ^ p
            for kind in range(4):
                at = pl.ds(pl.multiple_of(head * d + kind * wide, 8), d)
                turned[at, :] = block[0, kind * d : (kind + 1) * d]
        g2[0:slots, :], g2[slots:, :] = split(turned[wide:, :].T)
        ah, al = split(turned[0:wide, :].T)
        oh, ol = split(o_ref[...])
        r = jnp.dot(jnp.concatenate([ah, al], axis=0), oh, preferred_element_type=F32)
        r2 = jnp.dot(ah, ol, preferred_element_type=F32)
        rows = lax.broadcasted_iota(jnp.int32, x_ref.shape, 0)
        projected = r[0:slots] + (r[slots:] + r2)
        mixed[...] = jnp.where(rows < count[0, 0], x_ref[...] + projected, 0.0)

    wh, wl = split(w_ref[...])
    r = jnp.dot(g2[...], wh, preferred_element_type=F32)
    r2 = jnp.dot(g2[0:slots, :], wl, preferred_element_type=F32)
    acc[step] = r[0:slots] + (r[slots:] + r2)

    @pl.when(step == pl.num_programs(0) - 1)
    def _():
        g = jnp.concatenate([acc[i] for i in range(acc.shape[0])], axis=1)[:, 0:width]
        normed, inv_std = layer_norm(x_ref[...])
        mean = jnp.sum(g, axis=1, keepdims=True) / width
        along = jnp.sum(g * normed, axis=1, keepdims=True) / width
        grad[...] = masked_rows(c_ref, count) + inv_std * (g - mean - normed * along)


def finish(where, count, x, c, blocks, w_t, w_out):
    slots, width = x.shape
    smem = pl.BlockSpec(memory_space=pltpu.SMEM)
    step = 512
    steps = -(-width // step)
    columns = w_t.shape[0]
    first = lambda a: pl.BlockSpec((1,) + a.shape[1:], lambda i: (0, 0, 0))
    return pl.pallas_call(
        finish_kernel,
        grid=(steps,),
        in_specs=[smem, smem, whole(x), whole(c)]
        + [first(b) for b in blocks]
        + [pl.BlockSpec((columns, step), lambda i: (0, i)), whole(w_out)],
        out_specs=[whole(x), whole(x)],
        out_shape=[jax.ShapeDtypeStruct(x.shape, F32)] * 2,
        scratch_shapes=[
            pltpu.VMEM((2 * slots, columns), BF16),
            pltpu.VMEM((steps, slots, step), F32),
            pltpu.VMEM((4 * HEADS * HEAD_DIM, slots), F32),
        ],
        compiler_params=pltpu.CompilerParams(vmem_limit_bytes=56 * 2**20),
        cost_estimate=pl.CostEstimate(flops=10**10, bytes_accessed=25 * 10**6, transcendentals=0),
        name="finish",
    )(where, count, x, c, *blocks, w_t, w_out)


def per_device(tokens, counts, w_qkv, w_out, cotangent):
    where = jnp.stack([lax.axis_index(a) for a in AXES]).astype(jnp.int32)
    x, c = tokens[0], cotangent[0]
    w_t = w_qkv.T
    early = front(EARLY, False, where, counts, x, c, w_t, w_out)
    *late, near, far = front(LATE, True, where, counts, x, c, w_t, w_out)
    blocks = exchange(early, late)
    blocks, far = lax.optimization_barrier((blocks, far))
    far = other_core(far)
    made = attention(blocks)
    back = exchange([made[p] for p in EARLY], [made[p] for p in LATE])
    passed = (2, 6)
    straight = lax.optimization_barrier([b for p, b in enumerate(back) if p not in passed])
    others = [other_core(b) for b in straight]
    for p in passed:
        others.insert(p, other_core(back[p]))
    sums = weight_grads(where, near, far, *back, *others)
    back, sums = lax.optimization_barrier((back, sums))
    outs = finish(where, counts, x, c, back, w_t, w_out)
    share, (mixed, grad_tokens) = sum_over_chips(sums[:3], sums[3:], outs)

    share = jnp.concatenate([share[: 15 * 11], share[168 : 168 + 7 * 11]], axis=0)
    share = share.reshape(22, 11, 128).transpose(1, 0, 2).reshape(11, 22 * 128)
    wide = 3 * HEADS * HEAD_DIM
    return (mixed[None], grad_tokens[None], share[:, :wide], share[:, wide:].T)


def solution(mesh):
    split_mesh = Mesh(mesh.devices.reshape(4, 2, 2, 2, 4), AXES)
    dp, ctx = ("z", "yh", "core"), CTX
    return jax.shard_map(
        per_device,
        mesh=split_mesh,
        in_specs=(P(dp, ctx, None), P(dp, ctx), P(), P(), P(dp, ctx, None)),
        out_specs=(
            P(dp, ctx, None),
            P(dp, ctx, None),
            P(dp + ctx, None),
            P(None, dp + ctx),
        ),
        check_vma=False,
    )
```

```python
import functools

import jax
import jax.numpy as jnp
import numpy as np
from jax import lax
from jax.experimental import pallas as pl
from jax.experimental.pallas import tpu as pltpu
from jax.sharding import Mesh, PartitionSpec as P

HEADS = 8
HEAD_DIM = 88
SCALE = 1.0 / np.sqrt(np.float32(HEAD_DIM))
F32 = jnp.float32
BF16 = jnp.bfloat16
AXES = ("z", "yh", "core", "yl", "x")
CTX = ("yl", "x")
FLIPS = ((3, 1), (1, 3))
PAIR = [(0, 1), (1, 0)]


def split(a):
    hi = a.astype(BF16)
    return hi, (a - hi.astype(F32)).astype(BF16)


def halves(a):
    hi = a.astype(BF16).astype(F32)
    return hi, a - hi


LEAST = 5
LANES = 128


def attention_kernel(*refs):
    ins, outs, scratch = refs[:8], refs[8:16], refs[16:]
    packed, rk, rv, kc, vc, s_ref, pp, ds, dk, dv = scratch
    d = HEAD_DIM
    n = ins[0].shape[2]
    live_row = 4 * d
    dot = functools.partial(jnp.dot, preferred_element_type=F32)
    group = lambda i: slice(i * LANES, (i + 1) * LANES)

    offset = [0]
    for block in ins:
        count = jnp.sum(block[0, live_row : live_row + 1]).astype(jnp.int32)
        offset.append(pl.multiple_of(offset[-1] + ((count + 7) & ~7), 8))
    top = lax.broadcasted_iota(jnp.int32, (8, n), 0) == 0
    zeros = lambda rows: jnp.zeros((rows, n), F32)
    for block, first in zip(ins, offset):
        r = block[0]
        one = jnp.where(top, 1.0, 0.0)
        dead = jnp.where(top, (r[live_row:] - 1.0) * 1e30, 0.0)
        pieces = [r[0:d], one, zeros(32), r[3 * d : 4 * d], zeros(40)]
        pieces += [r[d : 2 * d], dead, zeros(32), r[2 * d : 3 * d], zeros(40)]
        packed[pl.ds(first, n), :] = jnp.concatenate(pieces, axis=0).T
    lanes = lax.broadcasted_iota(jnp.int32, (n, 4 * LANES), 1)
    nothing = jnp.where(lanes == 2 * LANES + d, -1e30, 0.0)
    packed[pl.ds(offset[-1], n), :] = nothing
    used = jnp.maximum((offset[-1] + n - 1) // n, LEAST)
    for b in range(LEAST):

        @pl.when(offset[-1] <= b * n)
        def _(b=b):
            packed[b * n : (b + 1) * n, :] = nothing

    def at(b):
        return pl.ds(pl.multiple_of(b * n, n), n)

    def prepare(b, c):
        t = packed[at(b), 2 * LANES :].T
        for i, (wide, rows) in enumerate(((rk, kc), (rv, vc))):
            hi, lo = split(t[group(i)])
            wide[group(0), at(b)] = hi
            wide[group(1), at(b)] = hi
            wide[group(2), at(b)] = lo
            rows[at(b), group(0)], rows[at(b), group(1)] = split(packed[at(b), group(2 + i)])
        return c

    lax.fori_loop(0, used, prepare, 0)
    dk[...] = jnp.zeros_like(dk)
    dv[...] = jnp.zeros_like(dv)

    def stacked(a):
        hi, lo = halves(a.T)
        both = jnp.concatenate([hi[0:d], lo[0:d]], axis=0).astype(BF16)
        return jnp.concatenate([both, both], axis=1)

    def fold(a):
        a = a[0:n] + a[n:]
        return a[:, group(0)] + a[:, group(1)]

    def queries(blocks, j):
        keys = blocks * n
        cuts = (0, keys) if blocks != 7 else (0, keys - n, keys)
        spans = [slice(a, b) for a, b in zip(cuts, cuts[1:])]
        tiles = [slice(b * n, (b + 1) * n) for b in range(blocks)]
        q = packed[at(j), group(0)] * SCALE
        qh, ql = split(q)
        lq = jnp.concatenate([qh, ql, qh], axis=1)
        m = jnp.full((n, LANES), -1e30, F32)
        for t in tiles:
            s = dot(lq, rk[:, t])
            s_ref[:, t] = s
            m = jnp.maximum(m, jnp.maximum(s[:, group(0)], s[:, group(1)]))
        m = jnp.max(m, axis=1, keepdims=True)
        l = jnp.zeros((n, LANES), F32)
        for t in tiles:
            p = jnp.exp(s_ref[:, t] - m)
            s_ref[:, t] = p
            pp[0:n, t], pp[n:, t] = split(p)
            l = l + (p[:, group(0)] + p[:, group(1)])
        o = sum(dot(pp[:, s], vc[s, :]) for s in spans)
        rl = 1.0 / jnp.sum(l, axis=1, keepdims=True)
        o = fold(o) * rl
        g = packed[at(j), group(1)] * rl
        row_dot = jnp.sum(g * o, axis=1, keepdims=True)
        gh, gl = split(g)
        lg = jnp.concatenate([gh, gl, gh], axis=1)
        g2 = stacked(g)
        for s in spans:
            dv[:, s] += dot(g2, pp[:, s])
        for t in tiles:
            grad = s_ref[:, t] * (dot(lg, rv[:, t]) - row_dot)
            ds[0:n, t], ds[n:, t] = split(grad)
        q2 = stacked(q)
        for s in spans:
            dk[:, s] += dot(q2, ds[:, s])
        packed[at(j), group(0)] = o
        packed[at(j), group(1)] = fold(sum(dot(ds[:, s], kc[s, :]) for s in spans)) * SCALE

    def all_queries(blocks):
        def body(j, c):
            queries(blocks, j)
            return c

        lax.fori_loop(0, blocks, body, 0)

    for blocks in range(LEAST, 9):
        pl.when(used == blocks)(functools.partial(all_queries, blocks))

    def finish_keys(b, c):
        for i, ref in enumerate((dk, dv)):
            a = ref[:, at(b)]
            a = jnp.concatenate([a[0:d] + a[d:], zeros(40)], axis=0)
            packed[at(b), group(2 + i)] = a.T
        return c

    lax.fori_loop(0, used, finish_keys, 0)
    for block, first, out in zip(ins, offset, outs):
        rows = packed[pl.ds(first, n), :].T
        live = block[0, live_row : live_row + 1] > 0
        for k in range(4):
            out[0, k * d : (k + 1) * d] = jnp.where(live, rows[k * LANES : k * LANES + d], 0.0)


def attention(blocks):
    rows, n = blocks[0].shape[1:]
    d = HEAD_DIM
    total = 8 * n
    first = lambda a: pl.BlockSpec((1, rows, n), lambda i: (0, 0, 0))
    return pl.pallas_call(
        attention_kernel,
        grid=(1,),
        out_shape=[jax.ShapeDtypeStruct((1, 4 * d, n), F32)] * 8,
        in_specs=[first(b) for b in blocks],
        out_specs=[pl.BlockSpec((1, 4 * d, n), lambda i: (0, 0, 0))] * 8,
        scratch_shapes=[
            pltpu.VMEM((total + n, 4 * LANES), F32),
            pltpu.VMEM((3 * LANES, total), BF16),
            pltpu.VMEM((3 * LANES, total), BF16),
            pltpu.VMEM((total, 2 * LANES), BF16),
            pltpu.VMEM((total, 2 * LANES), BF16),
            pltpu.VMEM((n, total), F32),
            pltpu.VMEM((2 * n, total), BF16),
            pltpu.VMEM((2 * n, total), BF16),
            pltpu.VMEM((2 * d, total), F32),
            pltpu.VMEM((2 * d, total), F32),
        ],
        compiler_params=pltpu.CompilerParams(vmem_limit_bytes=52 * 2**20),
        name="attention",
    )(*blocks)


PART_TILES = (8, 7, 7)
PART_ROWS = (88, 80, 80)
PART_RINGS = ((2, 1, 0), (1, 0, 2), (0, 2, 1))


def weights_kernel(where, near, far, *refs):
    own, other, refs = refs[:8], refs[8:16], refs[16:]
    results, made, (n3, m3, g3, a3, w, grads, done) = refs[:6], refs[6:12], refs[12:]
    sends, keeps = made[:3], made[3:]
    d = HEAD_DIM
    half = near.shape[3]
    rows = near.shape[1] * d
    wide = HEADS * d
    z, yh, core, yl, x = [where[i] for i in range(5)]

    def keep(at, to, lo, pieces):
        for i, p in enumerate(pieces):
            h, l = split(p)
            for k in range(3):
                to[at, (2 * k + i) * half : (2 * k + i + 1) * half] = (h, l)[k == lo]

    keep(slice(0, rows), n3, 2, [r[0].reshape(rows, half) for r in (near, far)])
    keep(slice(0, rows), m3, 2, [r[1].reshape(rows, half) for r in (near, far)])
    for i, blocks in enumerate((own, other)):
        for p, block in enumerate(blocks):
            grads[(yl * 4 + x) ^ p, :, i * half : (i + 1) * half] = block[0]

    def prepare(kind):
        for pair in range(HEADS // 2):
            pieces = [
                jnp.concatenate(
                    [
                        grads[2 * pair + k, kind * d : (kind + 1) * d, i * half : (i + 1) * half]
                        for k in range(2)
                    ],
                    axis=0,
                )
                for i in range(2)
            ]
            first = ((kind - 1) * wide if kind else 0) + 2 * pair * d
            keep(slice(first, first + 2 * d), g3 if kind else a3, 1, pieces)

    prepare(1)
    prepare(2)
    w[:, 0:768] = dot_rows(n3[...], g3[0:768, :])
    prepare(3)
    w[:, 768:1536] = dot_rows(n3[...], g3[768:1536, :])
    prepare(0)
    w[:, 1536 : 3 * wide] = dot_rows(n3[...], g3[1536:, :])
    w[:, 3 * wide :] = dot_rows(m3[...], a3[...])

    for refs in (sends, keeps):
        for ref in refs[1:]:
            ref[:, :, :, 72:80, :] = jnp.zeros((2, 2, 8, 8, 128), F32)

    def bits(own, to):
        p = own ^ to
        first = jnp.where(core == 0, p >> 1, (p ^ (p >> 1)) & 1)
        return first, jnp.where(core == 0, to & 1, to >> 1)

    def scatter(part, tile, zy, carry):
        at = pl.ds(pl.multiple_of(zy * d, 8), d)
        r0, r1, r2 = PART_RINGS[part]
        z_bits = bits(z, zy >> 1)
        for c in range(8):
            y_bits = bits((yh << 1) | yl, ((zy & 1) << 1) | (c >> 2))
            x_bits = bits(x, c & 3)
            a = (z_bits[0], y_bits[0], x_bits[0])
            j = (z_bits[1] << 2) | (y_bits[1] << 1) | x_bits[1]

            def store(ref, a=a, j=j, c=c):
                for t in range(PART_TILES[part]):
                    block = w[at, (tile + t) * 128 : (tile + t + 1) * 128]
                    ref[a[r1], a[r2], j, t * 11 : (t + 1) * 11, :] = block[c * 11 : (c + 1) * 11]

            pl.when(a[r0] == 1)(functools.partial(store, sends[part]))
            pl.when(a[r0] == 0)(functools.partial(store, keeps[part]))
        return carry

    copies = [pltpu.make_async_copy(m, r, done.at[i]) for i, (m, r) in enumerate(zip(made, results))]
    for part in range(3):
        lax.fori_loop(0, 8, functools.partial(scatter, part, sum(PART_TILES[:part])), 0)
        copies[part].start()
        copies[3 + part].start()
    for copy in copies:
        copy.wait()


def weight_grads(where, *arrays):
    _, blocks, _, half = arrays[0].shape
    rows = blocks * HEAD_DIM
    wide = HEADS * HEAD_DIM
    vmem = pl.BlockSpec(memory_space=pltpu.VMEM)
    return pl.pallas_call(
        weights_kernel,
        in_specs=[pl.BlockSpec(memory_space=pltpu.SMEM)] + [vmem] * len(arrays),
        out_specs=[pl.BlockSpec(memory_space=pl.ANY)] * 6,
        out_shape=[jax.ShapeDtypeStruct((2, 2, 8, r, 128), F32) for r in PART_ROWS] * 2,
        scratch_shapes=[pltpu.VMEM((2, 2, 8, r, 128), F32) for r in PART_ROWS] * 2
        + [
            pltpu.VMEM((rows, 6 * half), BF16),
            pltpu.VMEM((rows, 6 * half), BF16),
            pltpu.VMEM((3 * wide, 6 * half), BF16),
            pltpu.VMEM((wide, 6 * half), BF16),
            pltpu.VMEM((rows, 4 * wide), F32),
            pltpu.VMEM((HEADS, 4 * HEAD_DIM, 2 * half), F32),
            pltpu.SemaphoreType.DMA((6,)),
        ],
        compiler_params=pltpu.CompilerParams(vmem_limit_bytes=56 * 2**20),
        name="weight_grads",
    )(where, *arrays)


def index_of(z, y, core, x):
    return (((z * 2 + (y >> 1)) * 2 + core) * 2 + (y & 1)) * 4 + x


def swap_over(piece, flips, which):
    pairs = []
    for z in range(4):
        for y in range(4):
            for core in range(2):
                f = FLIPS[core][which]
                for x in range(4):
                    to = index_of(z ^ (f * flips[0]), y ^ (f * flips[1]), core, x ^ (f * flips[2]))
                    pairs.append((index_of(z, y, core, x), to))
    return lax.ppermute(piece, AXES, pairs)


def sum_over_chips(sends, keeps, beside):
    flips = lambda r: [int(r == k) for k in range(3)]
    sent = lax.optimization_barrier(list(sends))
    got = [swap_over(s, flips(r[0]), 0) for s, r in zip(sent, PART_RINGS)]
    got, beside = lax.optimization_barrier((got, beside))
    kept = list(keeps)
    for step in (1, 2):
        sent = [k[1] + g[1] for k, g in zip(kept, got)]
        kept = [k[0] + g[0] for k, g in zip(kept, got)]
        got = [swap_over(s, flips(r[step]), 0) for s, r in zip(sent, PART_RINGS)]
    rest = jnp.concatenate([k + g for k, g in zip(kept, got)], axis=1)
    got = lax.all_to_all(rest, AXES, 0, 0, axis_index_groups=last_groups(), tiled=True)
    return jnp.sum(got, axis=0), beside


def last_groups():
    groups = {}
    for z in range(4):
        for y in range(4):
            for core in range(2):
                for x in range(4):
                    kept = lambda i: (i ^ (i >> 1)) & 1 if core else i >> 1
                    label = lambda i: i >> 1 if core else i & 1
                    key = (core, kept(z), kept(y), kept(x))
                    groups.setdefault(key, []).append(((label(z), label(y), label(x)), index_of(z, y, core, x)))
    return [[i for _, i in sorted(g)] for g in groups.values()]


def exchange(early, late):
    send = lambda a, p: lax.ppermute(a, CTX, [(i, i ^ p) for i in range(8)])
    b2, b6, b5, b7 = early
    g2, g6, r5, r7 = send(b2, 1), send(b6, 3), send(b5, 5), send(b7, 7)
    g2, g6, late = lax.optimization_barrier((g2, g6, late))
    b0, b1, b3, b4 = late
    f2, f6 = send(g2, 3), send(g6, 5)
    return [b0, send(b1, 1), f2, send(b3, 3), send(b4, 4), r5, f6, r7]


def other_core(a):
    return lax.ppermute(a, "core", PAIR)


def layer_norm(x):
    centred = x - jnp.sum(x, axis=1, keepdims=True) / x.shape[1]
    var = jnp.sum(centred * centred, axis=1, keepdims=True) / x.shape[1]
    inv_std = lax.rsqrt(var + 1e-06)
    return centred * inv_std, inv_std


def masked_rows(ref, count):
    rows = lax.broadcasted_iota(jnp.int32, ref.shape, 0)
    return jnp.where(rows < count[0, 0], ref[...], 0.0)


def dot_rows(a, b):
    return lax.dot_general(a, b, (((1,), (1,)), ((), ())), preferred_element_type=F32)


EARLY = (2, 6, 5, 7)
LATE = (0, 1, 3, 4)


def whole(a):
    return pl.BlockSpec(a.shape, lambda *i: (0,) * len(a.shape))


def front_kernel(features, where, count, x_ref, c_ref, q_ref, k_ref, v_ref, o_ref, *refs):
    messages, refs = refs[:4], refs[4:]
    nh, nl, mh, ml = refs[-4:]
    d = HEAD_DIM
    slots = x_ref.shape[0]
    step = pl.program_id(0)

    @pl.when(step == 0)
    def _():
        normed, _ = layer_norm(x_ref[...])
        masked = masked_rows(c_ref, count)
        nh[...], nl[...] = split(normed)
        mh[...], ml[...] = split(masked)
        if features:
            near, far, turned = refs[:3]
            core = where[2]
            for k, a in enumerate((normed, masked)):
                turned[...] = a.T
                for i in range(8):
                    for ref, c in ((near, core), (far, 1 - core)):
                        ref[k, i] = turned[pl.ds(pl.multiple_of((2 * i + c) * d, 8), d), :]

    def project(w, hi, lo):
        rows = w.shape[0]
        wh, wl = halves(w)
        both = dot_rows(jnp.concatenate([wh, wl], axis=0).astype(BF16), hi[...])
        return both[0:rows] + (both[rows:] + dot_rows(wh.astype(BF16), lo[...]))

    qkv = project(jnp.concatenate([q_ref[...], k_ref[...], v_ref[...]], axis=0), nh, nl)
    grads = project(o_ref[...], mh, ml)
    lanes = lax.broadcasted_iota(jnp.int32, (8, slots), 1)
    for i, message in enumerate(messages):

        @pl.when(step == i)
        def _(message=message):
            message[0, 0 : 3 * d, :] = qkv
            message[0, 3 * d : 4 * d, :] = grads
            message[0, 4 * d :, :] = (lanes < count[0, 0]).astype(F32)


def front(places, features, where, count, x, c, w_t, w_out):
    slots, width = x.shape
    d = HEAD_DIM

    def part(kind):
        def index(i, where, count):
            p = places[0]
            for k in range(1, 4):
                p = jnp.where(i == k, places[k], p)
            return kind * HEADS + ((where[3] * 4 + where[4]) ^ p), 0

        return pl.BlockSpec((d, width), index)

    outs = [jax.ShapeDtypeStruct((1, 4 * d + 8, slots), F32)] * 4
    scratch = [pltpu.VMEM((slots, width), BF16)] * 4
    if features:
        outs += [jax.ShapeDtypeStruct((2, 8, d, slots), F32)] * 2
        scratch = [pltpu.VMEM((width, slots), F32)] + scratch
    return pl.pallas_call(
        functools.partial(front_kernel, features),
        grid_spec=pltpu.PrefetchScalarGridSpec(
            num_scalar_prefetch=2,
            grid=(4,),
            in_specs=[whole(x), whole(c), part(0), part(1), part(2), part(0)],
            out_specs=[whole(a) for a in outs],
            scratch_shapes=scratch,
        ),
        out_shape=outs,
        compiler_params=pltpu.CompilerParams(vmem_limit_bytes=58 * 2**20),
        cost_estimate=pl.CostEstimate(flops=6 * 10**9, bytes_accessed=14 * 10**6, transcendentals=0),
        name="front",
    )(where, count, x, c, w_t, w_t, w_t, w_out)


def finish_kernel(where, count, x_ref, c_ref, *refs):
    blocks, (w_ref, o_ref, mixed, grad, g2, acc, turned) = refs[:8], refs[8:]
    d = HEAD_DIM
    wide = HEADS * d
    slots, width = x_ref.shape
    step = pl.program_id(0)

    @pl.when(step == 0)
    def _():
        for p, block in enumerate(blocks):
            head = (where[3] * 4 + where[4]) ^ p
            for kind in range(4):
                at = pl.ds(pl.multiple_of(head * d + kind * wide, 8), d)
                turned[at, :] = block[0, kind * d : (kind + 1) * d]
        g2[0:slots, :], g2[slots:, :] = split(turned[wide:, :].T)
        ah, al = split(turned[0:wide, :].T)
        oh, ol = split(o_ref[...])
        r = jnp.dot(jnp.concatenate([ah, al], axis=0), oh, preferred_element_type=F32)
        r2 = jnp.dot(ah, ol, preferred_element_type=F32)
        rows = lax.broadcasted_iota(jnp.int32, x_ref.shape, 0)
        projected = r[0:slots] + (r[slots:] + r2)
        mixed[...] = jnp.where(rows < count[0, 0], x_ref[...] + projected, 0.0)

    wh, wl = split(w_ref[...])
    r = jnp.dot(g2[...], wh, preferred_element_type=F32)
    r2 = jnp.dot(g2[0:slots, :], wl, preferred_element_type=F32)
    acc[step] = r[0:slots] + (r[slots:] + r2)

    @pl.when(step == pl.num_programs(0) - 1)
    def _():
        g = jnp.concatenate([acc[i] for i in range(acc.shape[0])], axis=1)[:, 0:width]
        normed, inv_std = layer_norm(x_ref[...])
        mean = jnp.sum(g, axis=1, keepdims=True) / width
        along = jnp.sum(g * normed, axis=1, keepdims=True) / width
        grad[...] = masked_rows(c_ref, count) + inv_std * (g - mean - normed * along)


def finish(where, count, x, c, blocks, w_t, w_out):
    slots, width = x.shape
    smem = pl.BlockSpec(memory_space=pltpu.SMEM)
    step = 512
    steps = -(-width // step)
    columns = w_t.shape[0]
    first = lambda a: pl.BlockSpec((1,) + a.shape[1:], lambda i: (0, 0, 0))
    return pl.pallas_call(
        finish_kernel,
        grid=(steps,),
        in_specs=[smem, smem, whole(x), whole(c)]
        + [first(b) for b in blocks]
        + [pl.BlockSpec((columns, step), lambda i: (0, i)), whole(w_out)],
        out_specs=[whole(x), whole(x)],
        out_shape=[jax.ShapeDtypeStruct(x.shape, F32)] * 2,
        scratch_shapes=[
            pltpu.VMEM((2 * slots, columns), BF16),
            pltpu.VMEM((steps, slots, step), F32),
            pltpu.VMEM((4 * HEADS * HEAD_DIM, slots), F32),
        ],
        compiler_params=pltpu.CompilerParams(vmem_limit_bytes=56 * 2**20),
        cost_estimate=pl.CostEstimate(flops=10**10, bytes_accessed=25 * 10**6, transcendentals=0),
        name="finish",
    )(where, count, x, c, *blocks, w_t, w_out)


def per_device(tokens, counts, w_qkv, w_out, cotangent):
    where = jnp.stack([lax.axis_index(a) for a in AXES]).astype(jnp.int32)
    x, c = tokens[0], cotangent[0]
    w_t = w_qkv.T
    early = front(EARLY, False, where, counts, x, c, w_t, w_out)
    *late, near, far = front(LATE, True, where, counts, x, c, w_t, w_out)
    blocks = exchange(early, late)
    blocks, far = lax.optimization_barrier((blocks, far))
    far = other_core(far)
    made = attention(blocks)
    back = exchange([made[p] for p in EARLY], [made[p] for p in LATE])
    passed = (2, 6)
    straight = lax.optimization_barrier([b for p, b in enumerate(back) if p not in passed])
    others = [other_core(b) for b in straight]
    for p in passed:
        others.insert(p, other_core(back[p]))
    sums = weight_grads(where, near, far, *back, *others)
    back, sums = lax.optimization_barrier((back, sums))
    outs = finish(where, counts, x, c, back, w_t, w_out)
    share, (mixed, grad_tokens) = sum_over_chips(sums[:3], sums[3:], outs)

    share = jnp.concatenate([share[: 15 * 11], share[168 : 168 + 7 * 11]], axis=0)
    share = share.reshape(22, 11, 128).transpose(1, 0, 2).reshape(11, 22 * 128)
    wide = 3 * HEADS * HEAD_DIM
    return (mixed[None], grad_tokens[None], share[:, :wide], share[:, wide:].T)


def solution(mesh):
    split_mesh = Mesh(mesh.devices.reshape(4, 2, 2, 2, 4), AXES)
    dp, ctx = ("z", "yh", "core"), CTX
    return jax.shard_map(
        per_device,
        mesh=split_mesh,
        in_specs=(P(dp, ctx, None), P(dp, ctx), P(), P(), P(dp, ctx, None)),
        out_specs=(
            P(dp, ctx, None),
            P(dp, ctx, None),
            P(dp + ctx, None),
            P(None, dp + ctx),
        ),
        check_vma=False,
    )
```

```python
import functools

import jax
import jax.numpy as jnp
import numpy as np
from jax import lax
from jax.experimental import pallas as pl
from jax.experimental.pallas import tpu as pltpu
from jax.sharding import Mesh, PartitionSpec as P

HEADS = 8
HEAD_DIM = 88
SCALE = 1.0 / np.sqrt(np.float32(HEAD_DIM))
F32 = jnp.float32
BF16 = jnp.bfloat16
AXES = ("z", "yh", "core", "yl", "x")
CTX = ("yl", "x")
FLIPS = ((3, 1), (1, 3))
PAIR = [(0, 1), (1, 0)]


def split(a):
    hi = a.astype(BF16)
    return hi, (a - hi.astype(F32)).astype(BF16)


def halves(a):
    hi = a.astype(BF16).astype(F32)
    return hi, a - hi


LEAST = 5
LANES = 128


def attention_kernel(*refs):
    ins, outs, scratch = refs[:8], refs[8:16], refs[16:]
    packed, rk, rv, kc, vc, s_ref, pp, ds, dk, dv = scratch
    d = HEAD_DIM
    n = ins[0].shape[2]
    live_row = 4 * d
    dot = functools.partial(jnp.dot, preferred_element_type=F32)
    group = lambda i: slice(i * LANES, (i + 1) * LANES)

    offset = [0]
    for block in ins:
        count = jnp.sum(block[0, live_row : live_row + 1]).astype(jnp.int32)
        offset.append(pl.multiple_of(offset[-1] + ((count + 7) & ~7), 8))
    top = lax.broadcasted_iota(jnp.int32, (8, n), 0) == 0
    zeros = lambda rows: jnp.zeros((rows, n), F32)
    for block, first in zip(ins, offset):
        r = block[0]
        one = jnp.where(top, 1.0, 0.0)
        dead = jnp.where(top, (r[live_row:] - 1.0) * 1e30, 0.0)
        pieces = [r[0:d], one, zeros(32), r[3 * d : 4 * d], zeros(40)]
        pieces += [r[d : 2 * d], dead, zeros(32), r[2 * d : 3 * d], zeros(40)]
        packed[pl.ds(first, n), :] = jnp.concatenate(pieces, axis=0).T
    lanes = lax.broadcasted_iota(jnp.int32, (n, 4 * LANES), 1)
    nothing = jnp.where(lanes == 2 * LANES + d, -1e30, 0.0)
    packed[pl.ds(offset[-1], n), :] = nothing
    used = jnp.maximum((offset[-1] + n - 1) // n, LEAST)
    for b in range(LEAST):

        @pl.when(offset[-1] <= b * n)
        def _(b=b):
            packed[b * n : (b + 1) * n, :] = nothing

    def at(b):
        return pl.ds(pl.multiple_of(b * n, n), n)

    def prepare(b, c):
        t = packed[at(b), 2 * LANES :].T
        for i, (wide, rows) in enumerate(((rk, kc), (rv, vc))):
            hi, lo = split(t[group(i)])
            wide[group(0), at(b)] = hi
            wide[group(1), at(b)] = hi
            wide[group(2), at(b)] = lo
            rows[at(b), group(0)], rows[at(b), group(1)] = split(packed[at(b), group(2 + i)])
        return c

    lax.fori_loop(0, used, prepare, 0)
    dk[...] = jnp.zeros_like(dk)
    dv[...] = jnp.zeros_like(dv)

    def stacked(a):
        hi, lo = halves(a.T)
        both = jnp.concatenate([hi[0:d], lo[0:d]], axis=0).astype(BF16)
        return jnp.concatenate([both, both], axis=1)

    def fold(a):
        a = a[0:n] + a[n:]
        return a[:, group(0)] + a[:, group(1)]

    def queries(blocks, j):
        keys = blocks * n
        cuts = (0, keys) if blocks != 7 else (0, keys - n, keys)
        spans = [slice(a, b) for a, b in zip(cuts, cuts[1:])]
        tiles = [slice(b * n, (b + 1) * n) for b in range(blocks)]
        q = packed[at(j), group(0)] * SCALE
        qh, ql = split(q)
        lq = jnp.concatenate([qh, ql, qh], axis=1)
        m = jnp.full((n, LANES), -1e30, F32)
        for t in tiles:
            s = dot(lq, rk[:, t])
            s_ref[:, t] = s
            m = jnp.maximum(m, jnp.maximum(s[:, group(0)], s[:, group(1)]))
        m = jnp.max(m, axis=1, keepdims=True)
        l = jnp.zeros((n, LANES), F32)
        for t in tiles:
            p = jnp.exp(s_ref[:, t] - m)
            s_ref[:, t] = p
            pp[0:n, t], pp[n:, t] = split(p)
            l = l + (p[:, group(0)] + p[:, group(1)])
        o = sum(dot(pp[:, s], vc[s, :]) for s in spans)
        rl = 1.0 / jnp.sum(l, axis=1, keepdims=True)
        o = fold(o) * rl
        g = packed[at(j), group(1)] * rl
        row_dot = jnp.sum(g * o, axis=1, keepdims=True)
        gh, gl = split(g)
        lg = jnp.concatenate([gh, gl, gh], axis=1)
        g2 = stacked(g)
        for s in spans:
            dv[:, s] += dot(g2, pp[:, s])
        for t in tiles:
            grad = s_ref[:, t] * (dot(lg, rv[:, t]) - row_dot)
            ds[0:n, t], ds[n:, t] = split(grad)
        q2 = stacked(q)
        for s in spans:
            dk[:, s] += dot(q2, ds[:, s])
        packed[at(j), group(0)] = o
        packed[at(j), group(1)] = fold(sum(dot(ds[:, s], kc[s, :]) for s in spans)) * SCALE

    def all_queries(blocks):
        def body(j, c):
            queries(blocks, j)
            return c

        lax.fori_loop(0, blocks, body, 0)

    for blocks in range(LEAST, 9):
        pl.when(used == blocks)(functools.partial(all_queries, blocks))

    def finish_keys(b, c):
        for i, ref in enumerate((dk, dv)):
            a = ref[:, at(b)]
            a = jnp.concatenate([a[0:d] + a[d:], zeros(40)], axis=0)
            packed[at(b), group(2 + i)] = a.T
        return c

    lax.fori_loop(0, used, finish_keys, 0)
    for block, first, out in zip(ins, offset, outs):
        rows = packed[pl.ds(first, n), :].T
        live = block[0, live_row : live_row + 1] > 0
        for k in range(4):
            out[0, k * d : (k + 1) * d] = jnp.where(live, rows[k * LANES : k * LANES + d], 0.0)


def attention(blocks):
    rows, n = blocks[0].shape[1:]
    d = HEAD_DIM
    total = 8 * n
    first = lambda a: pl.BlockSpec((1, rows, n), lambda i: (0, 0, 0))
    return pl.pallas_call(
        attention_kernel,
        grid=(1,),
        out_shape=[jax.ShapeDtypeStruct((1, 4 * d, n), F32)] * 8,
        in_specs=[first(b) for b in blocks],
        out_specs=[pl.BlockSpec((1, 4 * d, n), lambda i: (0, 0, 0))] * 8,
        scratch_shapes=[
            pltpu.VMEM((total + n, 4 * LANES), F32),
            pltpu.VMEM((3 * LANES, total), BF16),
            pltpu.VMEM((3 * LANES, total), BF16),
            pltpu.VMEM((total, 2 * LANES), BF16),
            pltpu.VMEM((total, 2 * LANES), BF16),
            pltpu.VMEM((n, total), F32),
            pltpu.VMEM((2 * n, total), BF16),
            pltpu.VMEM((2 * n, total), BF16),
            pltpu.VMEM((2 * d, total), F32),
            pltpu.VMEM((2 * d, total), F32),
        ],
        compiler_params=pltpu.CompilerParams(vmem_limit_bytes=52 * 2**20),
        name="attention",
    )(*blocks)


PART_TILES = (8, 7, 7)
PART_ROWS = (88, 80, 80)
PART_RINGS = ((2, 1, 0), (1, 0, 2), (0, 2, 1))


def weights_kernel(where, near, far, *refs):
    own, other, refs = refs[:8], refs[8:16], refs[16:]
    results, made, (n3, m3, g3, a3, w, grads, done) = refs[:6], refs[6:12], refs[12:]
    sends, keeps = made[:3], made[3:]
    d = HEAD_DIM
    half = near.shape[3]
    rows = near.shape[1] * d
    wide = HEADS * d
    z, yh, core, yl, x = [where[i] for i in range(5)]

    def keep(at, to, lo, pieces):
        for i, p in enumerate(pieces):
            h, l = split(p)
            for k in range(3):
                to[at, (2 * k + i) * half : (2 * k + i + 1) * half] = (h, l)[k == lo]

    keep(slice(0, rows), n3, 2, [r[0].reshape(rows, half) for r in (near, far)])
    keep(slice(0, rows), m3, 2, [r[1].reshape(rows, half) for r in (near, far)])
    for i, blocks in enumerate((own, other)):
        for p, block in enumerate(blocks):
            grads[(yl * 4 + x) ^ p, :, i * half : (i + 1) * half] = block[0]

    def prepare(kind):
        for pair in range(HEADS // 2):
            pieces = [
                jnp.concatenate(
                    [
                        grads[2 * pair + k, kind * d : (kind + 1) * d, i * half : (i + 1) * half]
                        for k in range(2)
                    ],
                    axis=0,
                )
                for i in range(2)
            ]
            first = ((kind - 1) * wide if kind else 0) + 2 * pair * d
            keep(slice(first, first + 2 * d), g3 if kind else a3, 1, pieces)

    prepare(1)
    prepare(2)
    w[:, 0:768] = dot_rows(n3[...], g3[0:768, :])
    prepare(3)
    w[:, 768:1536] = dot_rows(n3[...], g3[768:1536, :])
    prepare(0)
    w[:, 1536 : 3 * wide] = dot_rows(n3[...], g3[1536:, :])
    w[:, 3 * wide :] = dot_rows(m3[...], a3[...])

    for refs in (sends, keeps):
        for ref in refs[1:]:
            ref[:, :, :, 72:80, :] = jnp.zeros((2, 2, 8, 8, 128), F32)

    def bits(own, to):
        p = own ^ to
        first = jnp.where(core == 0, p >> 1, (p ^ (p >> 1)) & 1)
        return first, jnp.where(core == 0, to & 1, to >> 1)

    def scatter(part, tile, zy, carry):
        at = pl.ds(pl.multiple_of(zy * d, 8), d)
        r0, r1, r2 = PART_RINGS[part]
        z_bits = bits(z, zy >> 1)
        for c in range(8):
            y_bits = bits((yh << 1) | yl, ((zy & 1) << 1) | (c >> 2))
            x_bits = bits(x, c & 3)
            a = (z_bits[0], y_bits[0], x_bits[0])
            j = (z_bits[1] << 2) | (y_bits[1] << 1) | x_bits[1]

            def store(ref, a=a, j=j, c=c):
                for t in range(PART_TILES[part]):
                    block = w[at, (tile + t) * 128 : (tile + t + 1) * 128]
                    ref[a[r1], a[r2], j, t * 11 : (t + 1) * 11, :] = block[c * 11 : (c + 1) * 11]

            pl.when(a[r0] == 1)(functools.partial(store, sends[part]))
            pl.when(a[r0] == 0)(functools.partial(store, keeps[part]))
        return carry

    copies = [pltpu.make_async_copy(m, r, done.at[i]) for i, (m, r) in enumerate(zip(made, results))]
    for part in range(3):
        lax.fori_loop(0, 8, functools.partial(scatter, part, sum(PART_TILES[:part])), 0)
        copies[part].start()
        copies[3 + part].start()
    for copy in copies:
        copy.wait()


def weight_grads(where, *arrays):
    _, blocks, _, half = arrays[0].shape
    rows = blocks * HEAD_DIM
    wide = HEADS * HEAD_DIM
    vmem = pl.BlockSpec(memory_space=pltpu.VMEM)
    return pl.pallas_call(
        weights_kernel,
        in_specs=[pl.BlockSpec(memory_space=pltpu.SMEM)] + [vmem] * len(arrays),
        out_specs=[pl.BlockSpec(memory_space=pl.ANY)] * 6,
        out_shape=[jax.ShapeDtypeStruct((2, 2, 8, r, 128), F32) for r in PART_ROWS] * 2,
        scratch_shapes=[pltpu.VMEM((2, 2, 8, r, 128), F32) for r in PART_ROWS] * 2
        + [
            pltpu.VMEM((rows, 6 * half), BF16),
            pltpu.VMEM((rows, 6 * half), BF16),
            pltpu.VMEM((3 * wide, 6 * half), BF16),
            pltpu.VMEM((wide, 6 * half), BF16),
            pltpu.VMEM((rows, 4 * wide), F32),
            pltpu.VMEM((HEADS, 4 * HEAD_DIM, 2 * half), F32),
            pltpu.SemaphoreType.DMA((6,)),
        ],
        compiler_params=pltpu.CompilerParams(vmem_limit_bytes=56 * 2**20),
        name="weight_grads",
    )(where, *arrays)


def index_of(z, y, core, x):
    return (((z * 2 + (y >> 1)) * 2 + core) * 2 + (y & 1)) * 4 + x


def swap_over(piece, flips, which):
    pairs = []
    for z in range(4):
        for y in range(4):
            for core in range(2):
                f = FLIPS[core][which]
                for x in range(4):
                    to = index_of(z ^ (f * flips[0]), y ^ (f * flips[1]), core, x ^ (f * flips[2]))
                    pairs.append((index_of(z, y, core, x), to))
    return lax.ppermute(piece, AXES, pairs)


def sum_over_chips(sends, keeps, beside):
    flips = lambda r: [int(r == k) for k in range(3)]
    sent = lax.optimization_barrier(list(sends))
    got = [swap_over(s, flips(r[0]), 0) for s, r in zip(sent, PART_RINGS)]
    got, beside = lax.optimization_barrier((got, beside))
    kept = list(keeps)
    for step in (1, 2):
        sent = [k[1] + g[1] for k, g in zip(kept, got)]
        kept = [k[0] + g[0] for k, g in zip(kept, got)]
        got = [swap_over(s, flips(r[step]), 0) for s, r in zip(sent, PART_RINGS)]
    rest = jnp.concatenate([k + g for k, g in zip(kept, got)], axis=1)
    got = lax.all_to_all(rest, AXES, 0, 0, axis_index_groups=last_groups(), tiled=True)
    return jnp.sum(got, axis=0), beside


def last_groups():
    groups = {}
    for z in range(4):
        for y in range(4):
            for core in range(2):
                for x in range(4):
                    kept = lambda i: (i ^ (i >> 1)) & 1 if core else i >> 1
                    label = lambda i: i >> 1 if core else i & 1
                    key = (core, kept(z), kept(y), kept(x))
                    groups.setdefault(key, []).append(((label(z), label(y), label(x)), index_of(z, y, core, x)))
    return [[i for _, i in sorted(g)] for g in groups.values()]


def exchange(early, late):
    send = lambda a, p: lax.ppermute(a, CTX, [(i, i ^ p) for i in range(8)])
    b2, b6, b5, b7 = early
    g2, g6, r5, r7 = send(b2, 1), send(b6, 3), send(b5, 5), send(b7, 7)
    g2, g6, late = lax.optimization_barrier((g2, g6, late))
    b0, b1, b3, b4 = late
    f2, f6 = send(g2, 3), send(g6, 5)
    return [b0, send(b1, 1), f2, send(b3, 3), send(b4, 4), r5, f6, r7]


def other_core(a):
    return lax.ppermute(a, "core", PAIR)


def layer_norm(x):
    centred = x - jnp.sum(x, axis=1, keepdims=True) / x.shape[1]
    var = jnp.sum(centred * centred, axis=1, keepdims=True) / x.shape[1]
    inv_std = lax.rsqrt(var + 1e-06)
    return centred * inv_std, inv_std


def masked_rows(ref, count):
    rows = lax.broadcasted_iota(jnp.int32, ref.shape, 0)
    return jnp.where(rows < count[0, 0], ref[...], 0.0)


def dot_rows(a, b):
    return lax.dot_general(a, b, (((1,), (1,)), ((), ())), preferred_element_type=F32)


EARLY = (2, 6, 5, 7)
LATE = (0, 1, 3, 4)


def whole(a):
    return pl.BlockSpec(a.shape, lambda *i: (0,) * len(a.shape))


def front_kernel(features, where, count, x_ref, c_ref, q_ref, k_ref, v_ref, o_ref, *refs):
    messages, refs = refs[:4], refs[4:]
    nh, nl, mh, ml = refs[-4:]
    d = HEAD_DIM
    slots = x_ref.shape[0]
    step = pl.program_id(0)

    @pl.when(step == 0)
    def _():
        normed, _ = layer_norm(x_ref[...])
        masked = masked_rows(c_ref, count)
        nh[...], nl[...] = split(normed)
        mh[...], ml[...] = split(masked)
        if features:
            near, far, turned = refs[:3]
            core = where[2]
            for k, a in enumerate((normed, masked)):
                turned[...] = a.T
                for i in range(8):
                    for ref, c in ((near, core), (far, 1 - core)):
                        ref[k, i] = turned[pl.ds(pl.multiple_of((2 * i + c) * d, 8), d), :]

    def project(w, hi, lo):
        rows = w.shape[0]
        wh, wl = halves(w)
        both = dot_rows(jnp.concatenate([wh, wl], axis=0).astype(BF16), hi[...])
        return both[0:rows] + (both[rows:] + dot_rows(wh.astype(BF16), lo[...]))

    qkv = project(jnp.concatenate([q_ref[...], k_ref[...], v_ref[...]], axis=0), nh, nl)
    grads = project(o_ref[...], mh, ml)
    lanes = lax.broadcasted_iota(jnp.int32, (8, slots), 1)
    for i, message in enumerate(messages):

        @pl.when(step == i)
        def _(message=message):
            message[0, 0 : 3 * d, :] = qkv
            message[0, 3 * d : 4 * d, :] = grads
            message[0, 4 * d :, :] = (lanes < count[0, 0]).astype(F32)


def front(places, features, where, count, x, c, w_t, w_out):
    slots, width = x.shape
    d = HEAD_DIM

    def part(kind):
        def index(i, where, count):
            p = places[0]
            for k in range(1, 4):
                p = jnp.where(i == k, places[k], p)
            return kind * HEADS + ((where[3] * 4 + where[4]) ^ p), 0

        return pl.BlockSpec((d, width), index)

    outs = [jax.ShapeDtypeStruct((1, 4 * d + 8, slots), F32)] * 4
    scratch = [pltpu.VMEM((slots, width), BF16)] * 4
    if features:
        outs += [jax.ShapeDtypeStruct((2, 8, d, slots), F32)] * 2
        scratch = [pltpu.VMEM((width, slots), F32)] + scratch
    return pl.pallas_call(
        functools.partial(front_kernel, features),
        grid_spec=pltpu.PrefetchScalarGridSpec(
            num_scalar_prefetch=2,
            grid=(4,),
            in_specs=[whole(x), whole(c), part(0), part(1), part(2), part(0)],
            out_specs=[whole(a) for a in outs],
            scratch_shapes=scratch,
        ),
        out_shape=outs,
        compiler_params=pltpu.CompilerParams(vmem_limit_bytes=58 * 2**20),
        cost_estimate=pl.CostEstimate(flops=6 * 10**9, bytes_accessed=14 * 10**6, transcendentals=0),
        name="front",
    )(where, count, x, c, w_t, w_t, w_t, w_out)


def finish_kernel(where, count, x_ref, c_ref, *refs):
    blocks, (w_ref, o_ref, mixed, grad, g2, acc, turned) = refs[:8], refs[8:]
    d = HEAD_DIM
    wide = HEADS * d
    slots, width = x_ref.shape
    step = pl.program_id(0)

    @pl.when(step == 0)
    def _():
        for p, block in enumerate(blocks):
            head = (where[3] * 4 + where[4]) ^ p
            for kind in range(4):
                at = pl.ds(pl.multiple_of(head * d + kind * wide, 8), d)
                turned[at, :] = block[0, kind * d : (kind + 1) * d]
        g2[0:slots, :], g2[slots:, :] = split(turned[wide:, :].T)
        ah, al = split(turned[0:wide, :].T)
        oh, ol = split(o_ref[...])
        r = jnp.dot(jnp.concatenate([ah, al], axis=0), oh, preferred_element_type=F32)
        r2 = jnp.dot(ah, ol, preferred_element_type=F32)
        rows = lax.broadcasted_iota(jnp.int32, x_ref.shape, 0)
        projected = r[0:slots] + (r[slots:] + r2)
        mixed[...] = jnp.where(rows < count[0, 0], x_ref[...] + projected, 0.0)

    wh, wl = split(w_ref[...])
    r = jnp.dot(g2[...], wh, preferred_element_type=F32)
    r2 = jnp.dot(g2[0:slots, :], wl, preferred_element_type=F32)
    acc[step] = r[0:slots] + (r[slots:] + r2)

    @pl.when(step == pl.num_programs(0) - 1)
    def _():
        g = jnp.concatenate([acc[i] for i in range(acc.shape[0])], axis=1)[:, 0:width]
        normed, inv_std = layer_norm(x_ref[...])
        mean = jnp.sum(g, axis=1, keepdims=True) / width
        along = jnp.sum(g * normed, axis=1, keepdims=True) / width
        grad[...] = masked_rows(c_ref, count) + inv_std * (g - mean - normed * along)


def finish(where, count, x, c, blocks, w_t, w_out):
    slots, width = x.shape
    smem = pl.BlockSpec(memory_space=pltpu.SMEM)
    step = 512
    steps = -(-width // step)
    columns = w_t.shape[0]
    first = lambda a: pl.BlockSpec((1,) + a.shape[1:], lambda i: (0, 0, 0))
    return pl.pallas_call(
        finish_kernel,
        grid=(steps,),
        in_specs=[smem, smem, whole(x), whole(c)]
        + [first(b) for b in blocks]
        + [pl.BlockSpec((columns, step), lambda i: (0, i)), whole(w_out)],
        out_specs=[whole(x), whole(x)],
        out_shape=[jax.ShapeDtypeStruct(x.shape, F32)] * 2,
        scratch_shapes=[
            pltpu.VMEM((2 * slots, columns), BF16),
            pltpu.VMEM((steps, slots, step), F32),
            pltpu.VMEM((4 * HEADS * HEAD_DIM, slots), F32),
        ],
        compiler_params=pltpu.CompilerParams(vmem_limit_bytes=56 * 2**20),
        cost_estimate=pl.CostEstimate(flops=10**10, bytes_accessed=25 * 10**6, transcendentals=0),
        name="finish",
    )(where, count, x, c, *blocks, w_t, w_out)


def per_device(tokens, counts, w_qkv, w_out, cotangent):
    where = jnp.stack([lax.axis_index(a) for a in AXES]).astype(jnp.int32)
    x, c = tokens[0], cotangent[0]
    w_t = w_qkv.T
    early = front(EARLY, False, where, counts, x, c, w_t, w_out)
    *late, near, far = front(LATE, True, where, counts, x, c, w_t, w_out)
    blocks = exchange(early, late)
    blocks, far = lax.optimization_barrier((blocks, far))
    far = other_core(far)
    made = attention(blocks)
    back = exchange([made[p] for p in EARLY], [made[p] for p in LATE])
    own_block, r1, r5, r7 = lax.optimization_barrier([back[p] for p in (0, 1, 5, 7)])
    r1, r3, r4 = lax.optimization_barrier([r1, back[3], back[4]])
    others = [other_core(b) for b in (own_block, r1, back[2], r3, r4, r5, back[6], r7)]
    sums = weight_grads(where, near, far, *back, *others)
    back, sums = lax.optimization_barrier((back, sums))
    outs = finish(where, counts, x, c, back, w_t, w_out)
    share, (mixed, grad_tokens) = sum_over_chips(sums[:3], sums[3:], outs)

    share = jnp.concatenate([share[: 15 * 11], share[168 : 168 + 7 * 11]], axis=0)
    share = share.reshape(22, 11, 128).transpose(1, 0, 2).reshape(11, 22 * 128)
    wide = 3 * HEADS * HEAD_DIM
    return (mixed[None], grad_tokens[None], share[:, :wide], share[:, wide:].T)


def solution(mesh):
    split_mesh = Mesh(mesh.devices.reshape(4, 2, 2, 2, 4), AXES)
    dp, ctx = ("z", "yh", "core"), CTX
    return jax.shard_map(
        per_device,
        mesh=split_mesh,
        in_specs=(P(dp, ctx, None), P(dp, ctx), P(), P(), P(dp, ctx, None)),
        out_specs=(
            P(dp, ctx, None),
            P(dp, ctx, None),
            P(dp + ctx, None),
            P(None, dp + ctx),
        ),
        check_vma=False,
    )
```
